512 devices in a mesh: seq: 64 (over z_lo, x, core), dp: 8 (over z_hi, y).
Axes of the slice: x: 4, y: 4, z: 16 (z_hi: 2, z_lo: 8; z = z_hi * 8 + z_lo), core: 2. Of those that a mesh axis runs over, the one named last changes fastest.
Arguments:
- layer_in: bfloat16 [4096, 16384], P('dp', 'seq'), may hold values from -6 to 6
- cotangent: bfloat16 [4096, 16384], P('dp', 'seq'), may hold values from -16 to 16
- value_taps: float32 [3, 4096], P(None, 'dp'), may hold values from -3.5 to 3.5
- gate_taps: float32 [3, 4096], P(None, 'dp'), may hold values from -3.5 to 3.5
- long_filter: bfloat16 [256, 16384], P('dp', 'seq'), may hold values from -2 to 2
Outputs:
- layer_out: bfloat16 [4096, 16384], P('dp', 'seq')
- input_grad: bfloat16 [4096, 16384], P('dp', 'seq')
- value_tap_grad: float32 [3, 4096], P(None, 'dp')
- gate_tap_grad: float32 [3, 4096], P(None, 'dp')
- filter_grad: float32 [256, 16384], P('dp', 'seq')
The draws below stay inside these ranges and needn't reach their ends.
All inputs are finite; a program needn't handle non-finite values.
Results may differ from the reference program's by a relative error of at most 0.0062.
Values may be sent and summed in bfloat16 or wider, within the bound.
A program may use at most 64 MiB of HBM per device.

```python
import jax
import jax.numpy as jnp
from jax import lax

C = 4096
GROUP = 16
G = 256
LENGTH = 16384


def draw_long_filter(key, part):
    key = jax.random.fold_in(key, 11)
    keys = jax.random.split(key, 3)
    reach = jnp.exp(jax.random.uniform(keys[0], (G, 1), jnp.float32, jnp.log(32.0), jnp.log(4.0 * LENGTH)))
    rough = jax.random.truncated_normal(keys[1], -4.0, 4.0, (G, LENGTH), jnp.float32)
    direct = jax.random.uniform(keys[2], (G, 1), jnp.float32, 0.3, 1.0)
    position = jnp.arange(LENGTH, dtype=jnp.float32)[None, :]
    amplitude = jnp.sqrt(2.0 / reach)
    first = jnp.where(position == 0.0, 1.0, 0.0)
    return (amplitude * rough * jnp.exp(-position / reach) + first * direct).astype(jnp.bfloat16)


def draw_cotangent(key, part):
    key = jax.random.fold_in(key, 23)
    keys = jax.random.split(key, 2)
    channel = jnp.arange(C, dtype=jnp.float32)[:, None] / C
    spread = jnp.exp(jax.random.uniform(keys[0], (C, 1), jnp.float32, jnp.log(0.3), jnp.log(3.0)))
    entries = jax.random.truncated_normal(keys[1], -4.0, 4.0, (C, LENGTH), jnp.float32)
    ramp = jnp.sqrt(0.4 + 1.2 * channel)
    return (entries * spread * ramp).astype(jnp.bfloat16)


def level_of(key, dims, pieces, low, top_value):
    def one(dim, blocks):
        steps = jax.random.uniform(jax.random.fold_in(jax.random.fold_in(key, 6), dim), (blocks,), jnp.float32, low / len(pieces), top_value / len(pieces))
        return jnp.repeat(jnp.exp(steps), dims[dim] // blocks).reshape((-1,) + (1,) * (len(dims) - dim - 1))

    gain = one(*pieces[0])
    for cut in pieces[1:]:
        gain = gain * one(*cut)
    return gain


def bell_draw(stream_key, dims, deviation, limit, shards=(), kind=jnp.bfloat16):
    array = deviation * jax.random.normal(stream_key, dims, jnp.float32)
    if shards:
        array = array * level_of(stream_key, dims, shards, -0.22, 0.18)
    return jnp.clip(array, -limit, limit).astype(kind)


def setup_inputs(seed: int = 0) -> dict:
    splits = jax.random.split(jax.random.key(seed), 6)
    layer_in = bell_draw(splits[0], (C, LENGTH), 1.0, 6.0, ((0, 8), (1, 64)))
    cotangent = draw_cotangent(jax.random.fold_in(splits[5], 71), 0)
    value_taps = bell_draw(splits[2], (3, C), 3 ** -0.5, 3.5, ((1, 8),), jnp.float32)
    gate_taps = bell_draw(splits[3], (3, C), 3 ** -0.5, 3.5, ((1, 8),), jnp.float32)
    long_filter = draw_long_filter(jax.random.fold_in(splits[5], 71), 0)
    return {"layer_in": layer_in, "cotangent": cotangent, "value_taps": value_taps, "gate_taps": gate_taps, "long_filter": long_filter}


def causal_mix(signal, taps):
    seq_len = signal.shape[1]
    padded = jnp.pad(signal, ((0, 0), (2, 0)))
    return taps[0][:, None] * padded[:, 2:2 + seq_len] + taps[1][:, None] * padded[:, 1:1 + seq_len] + taps[2][:, None] * padded[:, 0:seq_len]

def adjoint_mix(grad, taps):
    seq_len = grad.shape[1]
    padded = jnp.pad(grad, ((0, 0), (0, 2)))
    return taps[0][:, None] * padded[:, 0:seq_len] + taps[1][:, None] * padded[:, 1:1 + seq_len] + taps[2][:, None] * padded[:, 2:2 + seq_len]

def tap_terms(grad, signal):
    seq_len = signal.shape[1]
    padded = jnp.pad(signal, ((0, 0), (2, 0)))
    return jnp.stack([lax.optimization_barrier(jnp.sum(grad * padded[:, 2 - shift_by:2 - shift_by + seq_len], axis=1)) for shift_by in range(3)])

def one_group(items):
    values_g, grad_g, filt_g = items
    seq_len = values_g.shape[1]
    n_fft = 2 * seq_len
    value_spec = jnp.fft.rfft(values_g.astype(jnp.float32), n=n_fft, axis=1)
    grad_spec = jnp.fft.rfft(grad_g.astype(jnp.float32), n=n_fft, axis=1)
    filt_spec = jnp.fft.rfft(filt_g.astype(jnp.float32), n=n_fft)
    conv = jnp.fft.irfft(filt_spec[None, :] * value_spec, n=n_fft, axis=1)[:, :seq_len].astype(jnp.bfloat16)
    grad_s = jnp.fft.irfft(jnp.conj(filt_spec)[None, :] * grad_spec, n=n_fft, axis=1)[:, :seq_len].astype(jnp.bfloat16)
    cross = lax.optimization_barrier(jnp.sum(jnp.conj(value_spec) * grad_spec, axis=0))
    filt_part = jnp.fft.irfft(cross, n=n_fft)[:seq_len]
    return (conv, grad_s, filt_part)

def reference(layer_in, cotangent, value_taps, gate_taps, long_filter):
    wide_in = layer_in.astype(jnp.float32)
    upstream = cotangent.astype(jnp.float32)
    values = causal_mix(wide_in, value_taps).astype(jnp.bfloat16)
    gate = causal_mix(wide_in, gate_taps)
    grad_z = (gate * upstream).astype(jnp.bfloat16)
    conv, grad_s, filt_part = lax.map(one_group, (values.reshape(G, GROUP, LENGTH), grad_z.reshape(G, GROUP, LENGTH), long_filter))
    conv_wide = conv.reshape(C, LENGTH).astype(jnp.float32)
    grad_s_wide = grad_s.reshape(C, LENGTH).astype(jnp.float32)
    layer_out = (gate * conv_wide).astype(jnp.bfloat16)
    grad_g = (conv_wide * upstream).astype(jnp.bfloat16)
    grad_g_wide = grad_g.astype(jnp.float32)
    input_grad = (adjoint_mix(grad_s_wide, value_taps) + adjoint_mix(grad_g_wide, gate_taps)).astype(jnp.bfloat16)
    value_raw = tap_terms(grad_s_wide, wide_in)
    gate_raw = tap_terms(grad_g_wide, wide_in)
    total = jnp.sum(value_raw * value_raw) + jnp.sum(gate_raw * gate_raw)
    tap_norm = jnp.sqrt(total / jnp.float32(6 * C) + 1e-05)
    filter_grad = filt_part * (1.0 / jnp.sqrt(jnp.float32(GROUP * LENGTH)))
    return (layer_out, input_grad, value_raw / tap_norm, gate_raw / tap_norm, filter_grad)
```

```python
from functools import partial
import math

import jax
import jax.numpy as jnp
from jax import lax
from jax.experimental import pallas as pl
from jax.experimental.pallas import tpu as pltpu
from jax.sharding import PartitionSpec as P

GROUP = 16
LANES = 128
STACK = 4
MESH = pl.DeviceIdType.MESH
VMEM_LIMIT = 48 * 1024 * 1024
F32 = jnp.float32
BF16 = jnp.bfloat16


def greet(count):
    me = lax.axis_index("seq")
    barrier = pltpu.get_barrier_semaphore()

    @pl.loop(1, count)
    def _(step):
        peer = lax.rem(me + step, count)
        pl.semaphore_signal(barrier, inc=1, device_id={"seq": peer}, device_id_type=MESH)

    return barrier


def exchange_in(blocks, x_ref, u_ref, h_ref, xu_out, h_out, pack, got, hpack, hgot, sends, recvs):
    me = lax.axis_index("seq")
    barrier = greet(blocks)

    @pl.loop(0, blocks // 2)
    def _(pair):
        rows = pl.ds(pl.multiple_of(pair * 16, 16), 16)
        x = x_ref[rows, :].astype(F32)
        u = u_ref[rows, :].astype(F32)
        pack[2 * pair] = jnp.concatenate([x[:8], u[:8]], axis=0).astype(BF16)
        pack[2 * pair + 1] = jnp.concatenate([x[8:], u[8:]], axis=0).astype(BF16)

    taps = h_ref[...].astype(F32)
    for row in range(blocks // 2):
        hpack[row] = taps[row : row + 1]

    got[me] = pack[me]
    hgot[me] = hpack[me // 2]
    pl.semaphore_wait(barrier, blocks - 1)

    def copies(peer, source):
        return (
            pltpu.make_async_remote_copy(
                src_ref=hpack.at[peer // 2],
                dst_ref=hgot.at[source],
                send_sem=sends.at[0, peer],
                recv_sem=recvs.at[0, source],
                device_id={"seq": peer},
                device_id_type=MESH,
            ),
            pltpu.make_async_remote_copy(
                src_ref=pack.at[peer],
                dst_ref=got.at[source],
                send_sem=sends.at[1, peer],
                recv_sem=recvs.at[1, source],
                device_id={"seq": peer},
                device_id_type=MESH,
            ),
        )

    @pl.loop(1, blocks)
    def _(step):
        peer = lax.rem(me + step, blocks)
        for copy in copies(peer, me):
            copy.start()

    @pl.loop(1, blocks)
    def _(step):
        peer = lax.rem(me + step, blocks)
        for copy in copies(peer, peer):
            copy.wait_send()
            copy.wait_recv()

    xu_out[...] = got[...]
    h_out[...] = hgot[...]


def column(taps_ref, row, start):
    width = taps_ref.shape[1]
    wide = jnp.broadcast_to(taps_ref[row : row + 1, :], (8, width))
    lane = lax.broadcasted_iota(jnp.int32, (8, width), 1)
    chan = lax.broadcasted_iota(jnp.int32, (8, width), 0)
    return jnp.sum(jnp.where(lane == start + chan, wide, 0.0), axis=1, keepdims=True)


def long_work(blocks, scale, xu_ref, h_ref, vt_ref, gt_ref, o_ref, f_ref, t_ref, toep, stack, acc, v32, g32, gate, gp, fgs):
    cols = xu_ref.shape[2]
    me = lax.axis_index("seq")
    vt = [jnp.broadcast_to(column(vt_ref, j, me * 8), (8, cols)) for j in range(3)]
    gt = [jnp.broadcast_to(column(gt_ref, j, me * 8), (8, cols)) for j in range(3)]
    lane = lax.broadcasted_iota(jnp.int32, (8, cols), 1)
    sub_r = lax.broadcasted_iota(jnp.int32, (LANES, LANES), 0)
    sub_s = lax.broadcasted_iota(jnp.int32, (LANES, LANES), 1)
    full_r = lax.broadcasted_iota(jnp.int32, (cols, cols), 0)
    full_s = lax.broadcasted_iota(jnp.int32, (cols, cols), 1)
    flip = jnp.where(full_r + full_s == cols - 1, 1.0, 0.0).astype(BF16)

    def skew(block, half):
        row = h_ref[block, :, half * LANES : (half + 1) * LANES]
        return pltpu.roll(jnp.broadcast_to(row, (LANES, LANES)), 0, 1, stride=1, stride_axis=0)

    def build(block, carry):
        last_skew, last_edge = carry
        one, two = skew(block, 0), skew(block, 1)
        mid = jnp.where(sub_s >= sub_r, one, last_skew).astype(BF16)
        edge = jnp.where(sub_s >= sub_r, two, one).astype(BF16)
        toep[block, :LANES, :LANES] = mid
        toep[block, LANES:, LANES:] = mid
        toep[block, :LANES, LANES:] = edge
        toep[block, LANES:, :LANES] = last_edge
        return two, edge

    lax.fori_loop(
        0, blocks, build, (jnp.zeros((LANES, LANES), F32), jnp.zeros((LANES, LANES), BF16))
    )

    def short(block, carry):
        back1, back2 = carry
        both = xu_ref[block].astype(F32)
        x, u = both[:8], both[8:]
        roll1, roll2 = pltpu.roll(x, 1, 1), pltpu.roll(x, 2, 1)
        one = jnp.where(lane < 1, back1, roll1)
        two = jnp.where(lane < 2, back2, roll2)
        v32[block] = vt[0] * x + vt[1] * one + vt[2] * two
        g = gt[0] * x + gt[1] * one + gt[2] * two
        gate[block] = g
        g32[block] = g * u
        return roll1, roll2

    zero = jnp.zeros((8, cols), F32)
    lax.fori_loop(0, blocks, short, (zero, zero))

    rows = blocks * 8
    v16 = v32[...].reshape(rows, cols).astype(BF16)
    g16 = g32[...].reshape(rows, cols).astype(BF16)
    gp[0, :rows] = g16
    gp[0, rows:] = jnp.zeros((gp.shape[1] - rows, cols), BF16)
    gp[1, : rows - 16] = g32[1 : blocks - 1].reshape(rows - 16, cols).astype(BF16)
    gp[1, rows - 16 : rows] = jnp.concatenate([g32[blocks - 1], zero], axis=0).astype(BF16)
    gp[1, rows:] = jnp.zeros((gp.shape[1] - rows, cols), BF16)
    g32[...] = jnp.dot(g16, flip, preferred_element_type=F32).reshape(blocks, 8, cols)

    for shift in range(1, STACK):
        stack[:shift, :, shift * cols : (shift + 1) * cols] = jnp.zeros((shift, 16, cols), BF16)

    @pl.loop(0, blocks)
    def _(block):
        both = jnp.concatenate([v32[block], g32[blocks - 1 - block]], axis=0).astype(BF16)
        for shift in range(STACK):
            stack[block + shift, :, shift * cols : (shift + 1) * cols] = both

    for step in range(blocks // STACK):
        first = step * STACK
        left = stack[: blocks - first].reshape((blocks - first) * 16, STACK * cols)
        right = toep[first : first + STACK].reshape(STACK * cols, cols)
        part = jnp.dot(left, right, preferred_element_type=F32)
        part = part.reshape(blocks - first, 16, cols)
        if step == 0:
            acc[...] = part
        else:
            acc[first:] += part

    back = acc[:, 8:, :].reshape(rows, cols).astype(BF16)
    g32[...] = jnp.dot(back, flip, preferred_element_type=F32).reshape(blocks, 8, cols)

    def finish(step, carry):
        block = blocks - 1 - step
        nexts, sums = carry[:4], carry[4:]
        both = xu_ref[block].astype(F32)
        x, u = both[:8], both[8:]
        conv = acc[block, :8].astype(BF16).astype(F32)
        s0 = g32[step]
        c0 = (conv * u).astype(BF16).astype(F32)
        out = gate[block] * conv
        rolled = [pltpu.roll(s0, cols - 1, 1), pltpu.roll(s0, cols - 2, 1)]
        rolled += [pltpu.roll(c0, cols - 1, 1), pltpu.roll(c0, cols - 2, 1)]
        s1 = jnp.where(lane < cols - 1, rolled[0], nexts[0])
        s2 = jnp.where(lane < cols - 2, rolled[1], nexts[1])
        c1 = jnp.where(lane < cols - 1, rolled[2], nexts[2])
        c2 = jnp.where(lane < cols - 2, rolled[3], nexts[3])
        grad = vt[0] * s0 + vt[1] * s1 + vt[2] * s2 + (gt[0] * c0 + gt[1] * c1 + gt[2] * c2)
        o_ref[block] = jnp.concatenate([out, grad], axis=0).astype(BF16)
        terms = [s0, s1, s2, c0, c1, c2]
        return tuple(rolled) + tuple(a + t * x for a, t in zip(sums, terms))

    done = lax.fori_loop(0, blocks, finish, (zero,) * 10)
    spot = lax.broadcasted_iota(jnp.int32, (8, LANES), 1)
    chan = lax.broadcasted_iota(jnp.int32, (8, LANES), 0)
    row = jnp.zeros((8, LANES), F32)
    for j in range(6):
        total = jnp.sum(done[4 + j], axis=1, keepdims=True)
        row = jnp.where(spot == j * 8 + chan, jnp.broadcast_to(total, (8, LANES)), row)
    t_ref[...] = jnp.sum(row, axis=0, keepdims=True)

    v_flip = lax.dot_general(
        flip, v16, (((1,), (1,)), ((), ())), preferred_element_type=F32
    ).astype(BF16)
    upper = sub_r + sub_s >= LANES - 1

    def diagonal(tile):
        turned = pltpu.roll(tile, 1, 1, stride=1, stride_axis=0)
        return jnp.sum(turned, axis=0, keepdims=True) * scale

    def lag(depth, index, offset, parity, carry):
        last_mid, last_corner = carry
        right = gp[parity, pl.ds(pl.multiple_of(offset, 16), depth), :]
        prod = jnp.dot(v_flip[:, :depth], right, preferred_element_type=F32)
        edge = last_corner + prod[:LANES, :LANES]
        mid = prod[LANES:, :LANES] + prod[:LANES, LANES:]
        fgs[index, :, :LANES] = diagonal(jnp.where(upper, last_mid, edge))
        fgs[index, :, LANES:] = diagonal(jnp.where(upper, edge, mid))
        return mid, prod[LANES:, LANES:]

    def lags(depth, pair, carry):
        carry = lag(depth, 2 * pair, pair * 16, 0, carry)
        return lag(depth, 2 * pair + 1, pair * 16, 1, carry)

    carry = (jnp.zeros((LANES, LANES), F32),) * 2
    carry = lax.fori_loop(0, blocks // 4, partial(lags, rows), carry)
    carry = lax.fori_loop(blocks // 4, blocks // 2, partial(lags, rows // 2), carry)
    last_mid, last_corner = carry
    fgs[blocks, :, :LANES] = diagonal(jnp.where(upper, last_mid, last_corner))
    fgs[blocks, :, LANES:] = diagonal(jnp.where(upper, last_corner, 0.0))
    f_ref[...] = fgs[1:]


def exchange_out(
    blocks, replicas, o_ref, f_ref, t_ref, o_out, f_out, t_out,
    got, fx, fsum, fgot, tdp, trow, tgot, osem, orecv, xsem, fsem, frecv, dsem, drecv, tsem, trecv,
):
    me = lax.axis_index("seq")
    mine = lax.axis_index("dp")
    half = blocks // 2
    side = lax.rem(me, 2)
    sibling = me + 1 - 2 * side
    barrier = greet(blocks)

    @pl.loop(1, replicas)
    def _(step):
        peer = lax.rem(mine + step, replicas)
        pl.semaphore_signal(barrier, inc=1, device_id={"dp": peer}, device_id_type=MESH)

    raw = t_ref[...]
    lane = lax.broadcasted_iota(jnp.int32, (1, LANES), 1)
    squares = jnp.sum(jnp.where(lane < 48, raw * raw, 0.0), axis=1, keepdims=True)
    tdp[mine] = jnp.broadcast_to(squares, (1, LANES))
    got[me] = o_ref[me]
    pl.semaphore_wait(barrier, blocks + replicas - 2)

    def across(peer, source):
        return pltpu.make_async_remote_copy(
            src_ref=tdp.at[mine], dst_ref=tdp.at[source],
            send_sem=dsem.at[peer], recv_sem=drecv.at[source],
            device_id={"dp": peer}, device_id_type=MESH,
        )

    @pl.loop(1, replicas)
    def _(step):
        across(lax.rem(mine + step, replicas), mine).start()

    swap = pltpu.make_async_remote_copy(
        src_ref=f_ref.at[pl.ds((1 - side) * half, half)], dst_ref=fx,
        send_sem=xsem.at[0], recv_sem=xsem.at[1],
        device_id={"seq": sibling}, device_id_type=MESH,
    )
    swap.start()

    def main(peer, source):
        return pltpu.make_async_remote_copy(
            src_ref=o_ref.at[peer], dst_ref=got.at[source],
            send_sem=osem.at[peer], recv_sem=orecv.at[source],
            device_id={"seq": peer}, device_id_type=MESH,
        )

    @pl.loop(1, blocks)
    def _(step):
        main(lax.rem(me + step, blocks), me).start()

    @pl.loop(1, replicas)
    def _(step):
        peer = lax.rem(mine + step, replicas)
        across(peer, peer).wait_send()
        across(peer, peer).wait_recv()

    total = jnp.sum(tdp[...], axis=0)
    tgot[me] = jnp.where(lane < 48, raw, total)

    def around(peer, source):
        return pltpu.make_async_remote_copy(
            src_ref=tgot.at[me], dst_ref=tgot.at[source],
            send_sem=tsem.at[peer], recv_sem=trecv.at[source],
            device_id={"seq": peer}, device_id_type=MESH,
        )

    @pl.loop(1, blocks)
    def _(step):
        around(lax.rem(me + step, blocks), me).start()

    swap.wait()
    fsum[...] = f_ref[pl.ds(side * half, half)] + fx[...]

    def spread(index, peer, source):
        return pltpu.make_async_remote_copy(
            src_ref=fsum.at[index], dst_ref=fgot.at[source],
            send_sem=fsem.at[index], recv_sem=frecv.at[source],
            device_id={"seq": peer}, device_id_type=MESH,
        )

    home = me // half

    @pl.loop(0, half)
    def _(index):
        peer = side * half + index

        @pl.when(peer != me)
        def _():
            spread(index, peer, me // 2).start()

    @pl.when(home == side)
    def _():
        fgot[me // 2] = fsum[me - side * half]

    @pl.loop(0, half)
    def _(index):
        peer = side * half + index

        @pl.when(peer != me)
        def _():
            spread(index, peer, me // 2).wait_send()

        source = 2 * index + home

        @pl.when(source != me)
        def _():
            spread(index, peer, index).wait_recv()

    @pl.loop(1, blocks)
    def _(step):
        peer = lax.rem(me + step, blocks)
        main(peer, peer).wait_send()
        main(peer, peer).wait_recv()
        around(peer, peer).wait_send()
        around(peer, peer).wait_recv()

    o_out[...] = got[...]
    f_out[...] = fgot[...]
    t_out[...] = tgot[...]


def per_device(layer_in, cotangent, value_taps, gate_taps, long_filter):
    chans, cols = layer_in.shape
    blocks = lax.axis_size("seq")
    replicas = lax.axis_size("dp")
    half = blocks // 2
    scale = 1.0 / math.sqrt(GROUP * blocks * cols)
    vmem = pl.BlockSpec(memory_space=pltpu.VMEM)
    dma = pltpu.SemaphoreType.DMA
    both = jax.ShapeDtypeStruct((blocks, 16, cols), BF16)
    wide = jax.ShapeDtypeStruct((blocks, 1, cols), F32)
    xu, filt = pl.pallas_call(
        partial(exchange_in, blocks),
        out_shape=(both, wide),
        in_specs=[vmem] * 3,
        out_specs=(vmem, vmem),
        scratch_shapes=[
            pltpu.VMEM(both.shape, BF16),
            pltpu.VMEM(both.shape, BF16),
            pltpu.VMEM((half, 1, cols), F32),
            pltpu.VMEM(wide.shape, F32),
            dma((2, blocks)),
            dma((2, blocks)),
        ],
        compiler_params=pltpu.CompilerParams(
            collective_id=0, has_side_effects=True, vmem_limit_bytes=VMEM_LIMIT
        ),
        name="exchange_in",
    )(layer_in, cotangent, long_filter)
    out, filt_part, raw = pl.pallas_call(
        partial(long_work, blocks, scale),
        out_shape=(both, wide, jax.ShapeDtypeStruct((1, LANES), F32)),
        in_specs=[vmem] * 4,
        out_specs=(vmem,) * 3,
        scratch_shapes=[
            pltpu.VMEM((blocks, cols, cols), BF16),
            pltpu.VMEM((blocks + STACK, 16, STACK * cols), BF16),
            pltpu.VMEM((blocks, 16, cols), F32),
            pltpu.VMEM((blocks, 8, cols), F32),
            pltpu.VMEM((blocks, 8, cols), F32),
            pltpu.VMEM((blocks, 8, cols), F32),
            pltpu.VMEM((2, 2 * blocks * 8, cols), BF16),
            pltpu.VMEM((blocks + 1, 1, cols), F32),
        ],
        compiler_params=pltpu.CompilerParams(vmem_limit_bytes=VMEM_LIMIT),
        name="long_work",
    )(xu, filt, value_taps, gate_taps)
    got, filt_got, taps_got = pl.pallas_call(
        partial(exchange_out, blocks, replicas),
        out_shape=(
            both,
            jax.ShapeDtypeStruct((half, 1, cols), F32),
            jax.ShapeDtypeStruct((blocks, 1, LANES), F32),
        ),
        in_specs=[vmem] * 3,
        out_specs=(vmem,) * 3,
        scratch_shapes=[
            pltpu.VMEM(both.shape, BF16),
            pltpu.VMEM((half, 1, cols), F32),
            pltpu.VMEM((half, 1, cols), F32),
            pltpu.VMEM((half, 1, cols), F32),
            pltpu.VMEM((replicas, 1, LANES), F32),
            pltpu.VMEM((1, LANES), F32),
            pltpu.VMEM((blocks, 1, LANES), F32),
            dma((blocks,)),
            dma((blocks,)),
            dma((2,)),
            dma((half,)),
            dma((half,)),
            dma((replicas,)),
            dma((replicas,)),
            dma((blocks,)),
            dma((blocks,)),
        ],
        compiler_params=pltpu.CompilerParams(
            collective_id=1, has_side_effects=True, vmem_limit_bytes=VMEM_LIMIT
        ),
        name="exchange_out",
    )(out, filt_part, raw)
    parts = got.reshape(blocks, 2, 8, cols)
    layer_out = parts[:, 0].reshape(chans, cols)
    input_grad = parts[:, 1].reshape(chans, cols)
    rows = taps_got.reshape(blocks, LANES)
    total = jnp.sum(rows[:, 48])
    tap_scale = lax.rsqrt(total / F32(6 * chans * replicas) + 1e-05)
    taps = rows[:, :48].reshape(blocks, 6, 8).transpose(1, 0, 2).reshape(6, chans) * tap_scale
    return (layer_out, input_grad, taps[:3], taps[3:], filt_got.reshape(half, cols))


def solution(mesh):
    placed = (P("dp", "seq"), P("dp", "seq"), P(None, "dp"), P(None, "dp"), P("dp", "seq"))
    return jax.shard_map(
        per_device,
        mesh=mesh,
        in_specs=placed,
        out_specs=(P("dp", "seq"), P("dp", "seq"), P(None, "dp"), P(None, "dp"), P("dp", "seq")),
        check_vma=False,
    )
```

```python
from functools import partial
import math

import jax
import jax.numpy as jnp
from jax import lax
from jax.experimental import pallas as pl
from jax.experimental.pallas import tpu as pltpu
from jax.sharding import PartitionSpec as P

GROUP = 16
LANES = 128
STACK = 4
CHUNK = 8
MESH = pl.DeviceIdType.MESH
VMEM_LIMIT = 48 * 1024 * 1024
F32 = jnp.float32
BF16 = jnp.bfloat16


def widen(tile):
    wide = tile.astype(F32)
    return jnp.concatenate([wide[:, :8], wide[:, 8:]], axis=2)


def narrow(block):
    return jnp.concatenate([block[:, :, :LANES], block[:, :, LANES:]], axis=1).astype(BF16)


def to_messages(rows_ref, message_ref, blocks):
    @pl.loop(0, blocks // 2)
    def _(pair):
        rows = pl.ds(pl.multiple_of(pair * 16, 16), 16)
        wide = rows_ref[rows, :].astype(F32)
        message_ref[pl.ds(2 * pair, 2)] = narrow(wide.reshape(2, 8, 2 * LANES))


def from_messages(message_ref, rows_ref, blocks):
    @pl.loop(0, blocks // 2)
    def _(pair):
        rows = pl.ds(pl.multiple_of(pair * 16, 16), 16)
        wide = widen(message_ref[pl.ds(2 * pair, 2)])
        rows_ref[rows, :] = wide.reshape(16, 2 * LANES).astype(BF16)


def column(taps_ref, row, start):
    width = taps_ref.shape[1]
    wide = jnp.broadcast_to(taps_ref[row : row + 1, :], (8, width))
    lane = lax.broadcasted_iota(jnp.int32, (8, width), 1)
    chan = lax.broadcasted_iota(jnp.int32, (8, width), 0)
    return jnp.sum(jnp.where(lane == start + chan, wide, 0.0), axis=1, keepdims=True)


def fill_stack(load, stack, blocks, cols):
    for shift in range(2, STACK):
        stack[: shift // 2, :, shift * cols : (shift + 1) * cols] = jnp.zeros(
            (shift // 2, 16, cols), BF16
        )

    def body(pair, before):
        one, two = load(2 * pair), load(2 * pair + 1)
        even = jnp.concatenate([one, two], axis=0).astype(BF16)
        odd = jnp.concatenate([before, one], axis=0).astype(BF16)
        for shift in range(STACK):
            stack[pair + shift // 2, :, shift * cols : (shift + 1) * cols] = odd if shift % 2 else even
        return two

    lax.fori_loop(0, blocks // 2, body, jnp.zeros((8, cols), F32))


def long_conv(stack, toep, acc, blocks, cols):
    for step in range(blocks // STACK):
        first = step * STACK
        left = stack[: (blocks - first) // 2].reshape((blocks - first) * 8, STACK * cols)
        right = toep[first : first + STACK].reshape(STACK * cols, cols)
        part = jnp.dot(left, right, preferred_element_type=F32).reshape(blocks - first, 8, cols)
        if step == 0:
            acc[...] = part
        else:
            acc[first:] += part


def kernel(
    blocks, replicas, scale, norm,
    x_hbm, u_hbm, h_hbm, vt_hbm, gt_hbm,
    lo_out, ig_out, vt_out, gt_out, f_out,
    x_in, u_in, h_in, vt_ref, gt_ref,
    hpack, hgot, xpack, xgot, upack, ugot, lpack, lgot, ipack, igot,
    toep, stack, acc, v32, g32, gate, gp,
    fgs, fx, fsum, fgot, tdp, tgot, tall,
    loads, hsem, xsem, usem, lsem, isem, fsem, dsem, tsem,
):
    cols = x_hbm.shape[1]
    half = blocks // 2
    rows = blocks * 8
    me = lax.axis_index("seq")
    mine = lax.axis_index("dp")
    side = lax.rem(me, 2)
    chip = me // 2
    sibling = me + 1 - 2 * side

    barrier = pltpu.get_barrier_semaphore()

    @pl.loop(1, blocks)
    def _(step):
        peer = lax.rem(me + step, blocks)
        pl.semaphore_signal(barrier, inc=1, device_id={"seq": peer}, device_id_type=MESH)

    @pl.loop(1, replicas)
    def _(step):
        peer = lax.rem(mine + step, replicas)
        pl.semaphore_signal(barrier, inc=1, device_id={"dp": peer}, device_id_type=MESH)

    pairs = ((h_hbm, h_in), (x_hbm, x_in), (u_hbm, u_in), (vt_hbm, vt_ref), (gt_hbm, gt_ref))
    fetched = [pltpu.make_async_copy(a, b, loads.at[i]) for i, (a, b) in enumerate(pairs)]
    for copy in fetched:
        copy.start()

    def to_seq(source, target, sems, peer):
        return pltpu.make_async_remote_copy(
            src_ref=source, dst_ref=target, send_sem=sems.at[0], recv_sem=sems.at[1],
            device_id={"seq": peer}, device_id_type=MESH,
        )

    def send_all(pack, got, sems):
        @pl.loop(1, blocks)
        def _(step):
            peer = lax.rem(me + step, blocks)
            to_seq(pack.at[peer], got.at[me], sems, peer).start()

    def drain(ref, count, sem):
        part = ref.at[pl.ds(0, count)]
        pltpu.make_async_copy(part, part, sem).wait()

    fetched[0].wait()
    taps = h_in[...].astype(F32)
    for row in range(half):
        hpack[row] = taps[row : row + 1]
    hgot[side, chip] = hpack[chip]
    fetched[1].wait()
    to_messages(x_in, xpack, blocks)
    xgot[me] = xpack[me]
    fetched[2].wait()
    to_messages(u_in, upack, blocks)
    ugot[me] = upack[me]
    pl.semaphore_wait(barrier, blocks + replicas - 2)

    @pl.loop(1, half)
    def _(step):
        there = lax.rem(chip + step, half)
        to_seq(hpack.at[there], hgot.at[side, chip], hsem.at[0], 2 * there + side).start()

    send_all(xpack, xgot, xsem)
    drain(hgot.at[side], half - 1, hsem.at[0, 1])
    swap_h = to_seq(hgot.at[side], hgot.at[side], hsem.at[1], sibling)
    swap_h.start()
    send_all(upack, ugot, usem)

    fetched[3].wait()
    fetched[4].wait()
    vt = [jnp.broadcast_to(column(vt_ref, j, me * 8), (8, cols))[None] for j in range(3)]
    gt = [jnp.broadcast_to(column(gt_ref, j, me * 8), (8, cols))[None] for j in range(3)]
    lane = lax.broadcasted_iota(jnp.int32, (CHUNK, 8, cols), 2)
    sub_r = lax.broadcasted_iota(jnp.int32, (LANES, LANES), 0)
    sub_s = lax.broadcasted_iota(jnp.int32, (LANES, LANES), 1)
    full_r = lax.broadcasted_iota(jnp.int32, (cols, cols), 0)
    full_s = lax.broadcasted_iota(jnp.int32, (cols, cols), 1)
    flip = jnp.where(full_r + full_s == cols - 1, 1.0, 0.0).astype(BF16)
    zero = jnp.zeros((1, 8, cols), F32)
    swap_h.wait()

    def skew(block, part):
        row = hgot[lax.rem(block, 2), block // 2, :, part * LANES : (part + 1) * LANES]
        return pltpu.roll(jnp.broadcast_to(row, (LANES, LANES)), 0, 1, stride=1, stride_axis=0)

    def build(block, carry):
        last_skew, last_edge = carry
        one, two = skew(block, 0), skew(block, 1)
        mid = jnp.where(sub_s >= sub_r, one, last_skew).astype(BF16)
        edge = jnp.where(sub_s >= sub_r, two, one).astype(BF16)
        toep[block, :LANES, :LANES] = mid
        toep[block, LANES:, LANES:] = mid
        toep[block, :LANES, LANES:] = edge
        toep[block, LANES:, :LANES] = last_edge
        return two, edge

    lax.fori_loop(
        0, blocks, build, (jnp.zeros((LANES, LANES), F32), jnp.zeros((LANES, LANES), BF16))
    )

    drain(xgot, blocks - 1, xsem.at[1])

    def short(chunk, carry):
        part = pl.ds(chunk * CHUNK, CHUNK)
        x = widen(xgot[part])
        roll1, roll2 = pltpu.roll(x, 1, 2), pltpu.roll(x, 2, 2)
        one = jnp.where(lane < 1, jnp.concatenate([carry[0], roll1[:-1]], axis=0), roll1)
        two = jnp.where(lane < 2, jnp.concatenate([carry[1], roll2[:-1]], axis=0), roll2)
        v32[part] = vt[0] * x + vt[1] * one + vt[2] * two
        gate[part] = gt[0] * x + gt[1] * one + gt[2] * two
        return roll1[-1:], roll2[-1:]

    lax.fori_loop(0, blocks // CHUNK, short, (zero, zero))
    fill_stack(lambda block: v32[block], stack, blocks, cols)
    long_conv(stack, toep, acc, blocks, cols)

    @pl.loop(0, blocks // CHUNK)
    def _(chunk):
        part = pl.ds(chunk * CHUNK, CHUNK)
        conv = acc[part].astype(BF16).astype(F32)
        acc[part] = conv
        lpack[part] = narrow(gate[part] * conv)

    lgot[me] = lpack[me]
    send_all(lpack, lgot, lsem)

    drain(ugot, blocks - 1, usem.at[1])

    @pl.loop(0, blocks // CHUNK)
    def _(chunk):
        part = pl.ds(chunk * CHUNK, CHUNK)
        u = widen(ugot[part])
        g32[part] = gate[part] * u
        gate[part] = (acc[part] * u).astype(BF16).astype(F32)

    g16 = g32[...].reshape(rows, cols).astype(BF16)
    gp[0, :rows] = g16
    gp[0, rows:] = jnp.zeros((gp.shape[1] - rows, cols), BF16)
    gp[1, : rows - 16] = g32[1 : blocks - 1].reshape(rows - 16, cols).astype(BF16)
    gp[1, rows - 16 : rows] = jnp.concatenate(
        [g32[blocks - 1], jnp.zeros((8, cols), F32)], axis=0
    ).astype(BF16)
    gp[1, rows:] = jnp.zeros((gp.shape[1] - rows, cols), BF16)
    g32[...] = jnp.dot(g16, flip, preferred_element_type=F32).reshape(blocks, 8, cols)
    fill_stack(lambda block: g32[blocks - 1 - block], stack, blocks, cols)
    long_conv(stack, toep, acc, blocks, cols)
    back = acc[...].reshape(rows, cols).astype(BF16)
    g32[...] = jnp.dot(back, flip, preferred_element_type=F32).reshape(blocks, 8, cols)

    def finish(step, carry):
        first = (blocks // CHUNK - 1 - step) * CHUNK
        part = pl.ds(first, CHUNK)
        x = widen(xgot[part])
        s0 = jnp.concatenate(
            [g32[blocks - 1 - first - i][None] for i in range(CHUNK)], axis=0
        )
        c0 = gate[part]

        def ahead(wide, shift, after):
            turned = pltpu.roll(wide, cols - shift, 2)
            later = jnp.concatenate([turned[1:], after], axis=0)
            return jnp.where(lane < cols - shift, turned, later), turned[:1]

        s1, n0 = ahead(s0, 1, carry[0])
        s2, n1 = ahead(s0, 2, carry[1])
        c1, n2 = ahead(c0, 1, carry[2])
        c2, n3 = ahead(c0, 2, carry[3])
        grad = vt[0] * s0 + vt[1] * s1 + vt[2] * s2 + (gt[0] * c0 + gt[1] * c1 + gt[2] * c2)
        ipack[part] = narrow(grad)
        terms = [jnp.sum(t * x, axis=0, keepdims=True) for t in (s0, s1, s2, c0, c1, c2)]
        return (n0, n1, n2, n3) + tuple(a + t for a, t in zip(carry[4:], terms))

    done = lax.fori_loop(0, blocks // CHUNK, finish, (zero,) * 10)
    igot[me] = ipack[me]
    send_all(ipack, igot, isem)

    spot = lax.broadcasted_iota(jnp.int32, (8, LANES), 1)
    chan = lax.broadcasted_iota(jnp.int32, (8, LANES), 0)
    row = jnp.zeros((8, LANES), F32)
    for j in range(6):
        total = jnp.sum(done[4 + j][0], axis=1, keepdims=True)
        row = jnp.where(spot == j * 8 + chan, jnp.broadcast_to(total, (8, LANES)), row)
    raw = jnp.sum(row, axis=0, keepdims=True)
    squares = jnp.sum(raw * raw, axis=1, keepdims=True)
    tdp[mine] = jnp.broadcast_to(squares, (1, LANES))

    @pl.loop(1, replicas)
    def _(step):
        peer = lax.rem(mine + step, replicas)
        pltpu.make_async_remote_copy(
            src_ref=tdp.at[mine], dst_ref=tdp.at[mine], send_sem=dsem.at[0], recv_sem=dsem.at[1],
            device_id={"dp": peer}, device_id_type=MESH,
        ).start()

    v16 = v32[...].reshape(rows, cols).astype(BF16)
    v_flip = lax.dot_general(
        flip, v16, (((1,), (1,)), ((), ())), preferred_element_type=F32
    ).astype(BF16)
    upper = sub_r + sub_s >= LANES - 1

    def diagonal(tile):
        turned = pltpu.roll(tile, 1, 1, stride=1, stride_axis=0)
        return jnp.sum(turned, axis=0, keepdims=True) * scale

    def lag(depth, parity, pair, carry):
        last_mid, last_corner = carry
        right = gp[parity, pl.ds(pl.multiple_of(pair * 16, 16), depth), :]
        prod = jnp.dot(v_flip[:, :depth], right, preferred_element_type=F32)
        edge = last_corner + prod[:LANES, :LANES]
        mid = prod[LANES:, :LANES] + prod[:LANES, LANES:]
        index = pair if parity else pair
        fgs[parity, index, :, :LANES] = diagonal(jnp.where(upper, last_mid, edge))
        fgs[parity, index, :, LANES:] = diagonal(jnp.where(upper, edge, mid))
        return mid, prod[LANES:, LANES:]

    def lags(depth, pair, carry):
        return lag(depth, 1, pair, lag(depth, 0, pair, carry))

    carry = (jnp.zeros((LANES, LANES), F32),) * 2
    carry = lax.fori_loop(0, blocks // 4, partial(lags, rows), carry)
    carry = lax.fori_loop(blocks // 4, half, partial(lags, rows // 2), carry)
    last_mid, last_corner = carry
    fgs[0, half, :, :LANES] = diagonal(jnp.where(upper, last_mid, last_corner))
    fgs[0, half, :, LANES:] = diagonal(jnp.where(upper, last_corner, 0.0))

    swap_f = to_seq(fgs.at[side, pl.ds(1 - side, half)], fx, fsem.at[0], sibling)
    swap_f.start()

    drain(tdp, replicas - 1, dsem.at[0])
    drain(tdp, replicas - 1, dsem.at[1])
    total = tdp[0]
    for other in range(1, replicas):
        total = total + tdp[other]
    spot_row = lax.broadcasted_iota(jnp.int32, (1, LANES), 1)
    tgot[me] = jnp.where(spot_row < 48, raw, total)

    @pl.loop(1, blocks)
    def _(step):
        peer = lax.rem(me + step, blocks)
        to_seq(tgot.at[me], tgot.at[me], tsem, peer).start()

    swap_f.wait()
    fsum[...] = fgs[1 - side, pl.ds(side, half)] + fx[...]
    fgot[chip] = fsum[chip]

    @pl.loop(1, half)
    def _(step):
        there = lax.rem(chip + step, half)
        to_seq(fsum.at[there], fgot.at[chip], fsem.at[1], 2 * there + side).start()

    drain(lgot, blocks - 1, lsem.at[1])
    from_messages(lgot, lo_out, blocks)

    drain(tgot, blocks - 1, tsem.at[1])
    for block in range(blocks):
        tall[block : block + 1, :] = tgot[block]
    every = tall[...]
    total = jnp.sum(every[:, 48:49], axis=0, keepdims=True)
    factor = lax.rsqrt(total * norm + 1e-05)
    width = blocks * 8
    pick_k = lax.broadcasted_iota(jnp.int32, (LANES, width), 0)
    pick_l = lax.broadcasted_iota(jnp.int32, (LANES, width), 1)
    own_i = lax.broadcasted_iota(jnp.int32, (blocks, width), 0)
    own_l = lax.broadcasted_iota(jnp.int32, (blocks, width), 1)
    for j in range(6):
        pick = jnp.where(pick_k == 8 * j + lax.rem(pick_l, 8), 1.0, 0.0)
        spread = jnp.dot(every, pick, precision=lax.Precision.HIGHEST, preferred_element_type=F32)
        line = jnp.sum(jnp.where(own_i == own_l // 8, spread, 0.0), axis=0, keepdims=True)
        (gt_out if j >= 3 else vt_out)[j % 3 : j % 3 + 1, :] = line * factor

    drain(fgot, half - 1, fsem.at[1, 1])
    for block in range(half):
        f_out[block : block + 1, :] = fgot[block]
    drain(igot, blocks - 1, isem.at[1])
    from_messages(igot, ig_out, blocks)

    for ref, sems in ((xpack, xsem), (upack, usem), (lpack, lsem), (ipack, isem), (tgot, tsem)):
        drain(ref, blocks - 1, sems.at[0])
    drain(hpack, half - 1, hsem.at[0, 0])
    drain(fsum, half - 1, fsem.at[1, 0])


def per_device(layer_in, cotangent, value_taps, gate_taps, long_filter):
    chans, cols = layer_in.shape
    blocks = lax.axis_size("seq")
    replicas = lax.axis_size("dp")
    half = blocks // 2
    scale = 1.0 / math.sqrt(GROUP * blocks * cols)
    norm = 1.0 / (6 * chans * replicas)
    vmem = pl.BlockSpec(memory_space=pltpu.VMEM)
    anywhere = pl.BlockSpec(memory_space=pl.ANY)
    dma = pltpu.SemaphoreType.DMA
    message = pltpu.VMEM((blocks, 16, LANES), BF16)
    wide = pltpu.VMEM((blocks, 8, cols), F32)
    lines = pltpu.VMEM((half, 1, cols), F32)
    outs = pl.pallas_call(
        partial(kernel, blocks, replicas, scale, norm),
        out_shape=(
            jax.ShapeDtypeStruct((chans, cols), BF16),
            jax.ShapeDtypeStruct((chans, cols), BF16),
            jax.ShapeDtypeStruct((3, chans), F32),
            jax.ShapeDtypeStruct((3, chans), F32),
            jax.ShapeDtypeStruct((half, cols), F32),
        ),
        in_specs=[anywhere] * 5,
        out_specs=(vmem,) * 5,
        scratch_shapes=[
            pltpu.VMEM((chans, cols), BF16),
            pltpu.VMEM((chans, cols), BF16),
            pltpu.VMEM((half, cols), BF16),
            pltpu.VMEM((3, chans), F32),
            pltpu.VMEM((3, chans), F32),
            lines,
            pltpu.VMEM((2, half, 1, cols), F32),
            *([message] * 8),
            pltpu.VMEM((blocks, cols, cols), BF16),
            pltpu.VMEM((half + STACK // 2, 16, STACK * cols), BF16),
            *([wide] * 4),
            pltpu.VMEM((2, 2 * blocks * 8, cols), BF16),
            pltpu.VMEM((2, half + 1, 1, cols), F32),
            lines,
            lines,
            lines,
            pltpu.VMEM((replicas, 1, LANES), F32),
            pltpu.VMEM((blocks, 1, LANES), F32),
            pltpu.VMEM((blocks, LANES), F32),
            dma((5,)),
            dma((2, 2)),
            dma((2,)),
            dma((2,)),
            dma((2,)),
            dma((2,)),
            dma((2, 2)),
            dma((2,)),
            dma((2,)),
        ],
        compiler_params=pltpu.CompilerParams(
            collective_id=0, has_side_effects=True, vmem_limit_bytes=VMEM_LIMIT
        ),
        name="hyena",
    )(layer_in, cotangent, long_filter, value_taps, gate_taps)
    return outs


def solution(mesh):
    placed = (P("dp", "seq"), P("dp", "seq"), P(None, "dp"), P(None, "dp"), P("dp", "seq"))
    return jax.shard_map(
        per_device,
        mesh=mesh,
        in_specs=placed,
        out_specs=(P("dp", "seq"), P("dp", "seq"), P(None, "dp"), P(None, "dp"), P("dp", "seq")),
        check_vma=False,
    )
```

```python
from functools import partial
import math

import jax
import jax.numpy as jnp
from jax import lax
from jax.experimental import pallas as pl
from jax.experimental.pallas import tpu as pltpu
from jax.sharding import PartitionSpec as P

GROUP = 16
LANES = 128
STACK = 8
CHUNK = 8
UNROLL = 4
TURNS = 2
PART = 40
MESH = pl.DeviceIdType.MESH
VMEM_LIMIT = 60 * 1024 * 1024
F32 = jnp.float32
BF16 = jnp.bfloat16


def widen(tile):
    wide = tile.astype(F32)
    return jnp.concatenate([wide[:, :8], wide[:, 8:]], axis=2)


def narrow(block):
    return jnp.concatenate([block[:, :, :LANES], block[:, :, LANES:]], axis=1).astype(BF16)


def to_messages(rows_ref, message_ref, blocks):
    @pl.loop(0, blocks // 2)
    def _(pair):
        rows = pl.ds(pl.multiple_of(pair * 16, 16), 16)
        wide = rows_ref[rows, :].astype(F32)
        message_ref[pl.ds(2 * pair, 2)] = narrow(wide.reshape(2, 8, 2 * LANES))


def from_messages(message_ref, rows_ref, blocks):
    @pl.loop(0, blocks // 2)
    def _(pair):
        rows = pl.ds(pl.multiple_of(pair * 16, 16), 16)
        wide = widen(message_ref[pl.ds(2 * pair, 2)])
        rows_ref[rows, :] = wide.reshape(16, 2 * LANES).astype(BF16)


def column(taps_ref, row, start):
    width = taps_ref.shape[1]
    wide = jnp.broadcast_to(taps_ref[row : row + 1, :], (8, width))
    lane = lax.broadcasted_iota(jnp.int32, (8, width), 1)
    chan = lax.broadcasted_iota(jnp.int32, (8, width), 0)
    return jnp.sum(jnp.where(lane == start + chan, wide, 0.0), axis=1, keepdims=True)


def fill_stack(load, stack, blocks, cols):
    for shift in range(2, STACK):
        stack[: shift // 2, :, shift * cols : (shift + 1) * cols] = jnp.zeros(
            (shift // 2, 16, cols), BF16
        )

    def body(pair, before):
        one, two = load(2 * pair), load(2 * pair + 1)
        even = jnp.concatenate([one, two], axis=0).astype(BF16)
        odd = jnp.concatenate([before, one], axis=0).astype(BF16)
        for shift in range(STACK):
            stack[pair + shift // 2, :, shift * cols : (shift + 1) * cols] = odd if shift % 2 else even
        return two

    lax.fori_loop(0, blocks // 2, body, jnp.zeros((8, cols), F32))


def long_conv(stack, toep, acc, blocks, cols):
    turns = blocks // STACK
    acc[...] = jnp.zeros(acc.shape, F32)
    for start in range(0, turns, TURNS):
        depth = blocks - start * STACK
        left = stack[: depth // 2].reshape(depth * 8, STACK * cols)

        @pl.loop(start, start + TURNS)
        def _(turn):
            first = turn * STACK
            right = toep[pl.ds(first, STACK)].reshape(STACK * cols, cols)
            part = jnp.dot(left, right, preferred_element_type=F32).reshape(depth, 8, cols)
            acc[pl.ds(first, depth)] += part


def kernel(
    blocks, replicas, scale, norm,
    x_hbm, u_hbm, h_hbm, vt_hbm, gt_hbm,
    lgot, igot, fgot, t_out,
    x_in, u_in, h_in, vt_ref, gt_ref,
    hpack, hgot, xpack, xgot, upack, ugot, lpack, ipack,
    toep, stack, acc, v32, g32, r32, gate, gp,
    fgs, fx, fsum, twin, tdp, tnorm, tgot, tall, t_vmem,
    loads, hsem, xsem, usem, lsem, isem, fsem, dsem, tsem, own,
):
    cols = x_hbm.shape[1]
    half = blocks // 2
    rows = blocks * 8
    me = lax.axis_index("seq")
    mine = lax.axis_index("dp")
    side = lax.rem(me, 2)
    chip = me // 2
    sibling = me + 1 - 2 * side

    barrier = pltpu.get_barrier_semaphore()

    @pl.loop(1, blocks)
    def _(step):
        peer = lax.rem(me + step, blocks)
        pl.semaphore_signal(barrier, inc=1, device_id={"seq": peer}, device_id_type=MESH)

    lead = half

    @pl.when(me == lead)
    def _():
        @pl.loop(1, replicas)
        def _(step):
            peer = lax.rem(mine + step, replicas)
            pl.semaphore_signal(barrier, inc=1, device_id={"dp": peer}, device_id_type=MESH)

    pairs = ((h_hbm, h_in), (x_hbm, x_in), (u_hbm, u_in), (vt_hbm, vt_ref), (gt_hbm, gt_ref))
    fetched = [pltpu.make_async_copy(a, b, loads.at[i]) for i, (a, b) in enumerate(pairs)]
    for copy in fetched:
        copy.start()

    def to_seq(source, target, sems, peer):
        return pltpu.make_async_remote_copy(
            src_ref=source, dst_ref=target, send_sem=sems.at[0], recv_sem=sems.at[1],
            device_id={"seq": peer}, device_id_type=MESH,
        )

    def send_some(pack, got, sems, first, last):
        @pl.loop(first, last)
        def _(step):
            peer = lax.rem(me + step, blocks)
            to_seq(pack.at[peer], got.at[me], sems, peer).start()

    def drain(ref, count, sem):
        part = ref.at[pl.ds(0, count)]
        pltpu.make_async_copy(part, part, sem).wait()

    fetched[0].wait()
    taps = h_in[...].astype(F32)
    for row in range(half):
        hpack[row] = taps[row : row + 1]
    hgot[side, chip] = hpack[chip]
    fetched[1].wait()
    to_messages(x_in, xpack, blocks)
    xgot[me] = xpack[me]
    fetched[2].wait()
    to_messages(u_in, upack, blocks)
    ugot[me] = upack[me]
    pl.semaphore_wait(barrier, blocks - 1 + jnp.where(me == lead, replicas - 1, 0))

    @pl.loop(1, half)
    def _(step):
        there = lax.rem(chip + step, half)
        to_seq(hpack.at[there], hgot.at[side, chip], hsem.at[0], 2 * there + side).start()

    send_some(xpack, xgot, xsem, 1, blocks)
    drain(hgot.at[side], half - 1, hsem.at[0, 1])
    swap_h = to_seq(hgot.at[side], hgot.at[side], hsem.at[1], sibling)
    swap_h.start()
    send_some(upack, ugot, usem, 1, blocks)

    fetched[3].wait()
    fetched[4].wait()
    vt = [jnp.broadcast_to(column(vt_ref, j, me * 8), (8, cols))[None] for j in range(3)]
    gt = [jnp.broadcast_to(column(gt_ref, j, me * 8), (8, cols))[None] for j in range(3)]
    lane = lax.broadcasted_iota(jnp.int32, (CHUNK, 8, cols), 2)
    sub_r = lax.broadcasted_iota(jnp.int32, (LANES, LANES), 0)
    sub_s = lax.broadcasted_iota(jnp.int32, (LANES, LANES), 1)
    full_r = lax.broadcasted_iota(jnp.int32, (cols, cols), 0)
    full_s = lax.broadcasted_iota(jnp.int32, (cols, cols), 1)
    flip = jnp.where(full_r + full_s == cols - 1, 1.0, 0.0).astype(BF16)
    zero = jnp.zeros((1, 8, cols), F32)
    swap_h.wait()

    def skew(block, part):
        row = hgot[lax.rem(block, 2), block // 2, :, part * LANES : (part + 1) * LANES]
        return pltpu.roll(jnp.broadcast_to(row, (LANES, LANES)), 0, 1, stride=1, stride_axis=0)

    def build(group, carry):
        last_skew, last_edge = carry
        for i in range(UNROLL):
            block = group * UNROLL + i
            one, two = skew(block, 0), skew(block, 1)
            mid = jnp.where(sub_s >= sub_r, one, last_skew).astype(BF16)
            edge = jnp.where(sub_s >= sub_r, two, one).astype(BF16)
            toep[block, :LANES, :LANES] = mid
            toep[block, LANES:, LANES:] = mid
            toep[block, :LANES, LANES:] = edge
            toep[block, LANES:, :LANES] = last_edge
            last_skew, last_edge = two, edge
        return last_skew, last_edge

    lax.fori_loop(
        0,
        blocks // UNROLL,
        build,
        (jnp.zeros((LANES, LANES), F32), jnp.zeros((LANES, LANES), BF16)),
    )

    drain(xgot, blocks - 1, xsem.at[1])

    def short(chunk, carry):
        part = pl.ds(chunk * CHUNK, CHUNK)
        x = widen(xgot[part])
        roll1, roll2 = pltpu.roll(x, 1, 2), pltpu.roll(x, 2, 2)
        one = jnp.where(lane < 1, jnp.concatenate([carry[0], roll1[:-1]], axis=0), roll1)
        two = jnp.where(lane < 2, jnp.concatenate([carry[1], roll2[:-1]], axis=0), roll2)
        v32[part] = vt[0] * x + vt[1] * one + vt[2] * two
        gate[part] = gt[0] * x + gt[1] * one + gt[2] * two
        return roll1[-1:], roll2[-1:]

    lax.fori_loop(0, blocks // CHUNK, short, (zero, zero))
    fill_stack(lambda block: v32[block], stack, blocks, cols)
    long_conv(stack, toep, acc, blocks, cols)

    @pl.loop(0, blocks // CHUNK)
    def _(chunk):
        part = pl.ds(chunk * CHUNK, CHUNK)
        conv = acc[part].astype(BF16).astype(F32)
        acc[part] = conv
        lpack[part] = narrow(gate[part] * conv)

    keep_l = pltpu.make_async_copy(lpack.at[me], lgot.at[me], own.at[0])
    keep_l.start()
    send_some(lpack, lgot, lsem, 1, blocks)

    drain(ugot, blocks - 1, usem.at[1])

    @pl.loop(0, blocks // CHUNK)
    def _(chunk):
        part = pl.ds(chunk * CHUNK, CHUNK)
        u = widen(ugot[part])
        g32[part] = gate[part] * u
        gate[part] = (acc[part] * u).astype(BF16).astype(F32)

    g16 = g32[...].reshape(rows, cols).astype(BF16)
    r32[...] = jnp.dot(g16, flip, preferred_element_type=F32).reshape(blocks, 8, cols)
    fill_stack(lambda block: r32[blocks - 1 - block], stack, blocks, cols)
    long_conv(stack, toep, acc, blocks, cols)
    back = acc[:blocks].reshape(rows, cols).astype(BF16)
    r32[...] = jnp.dot(back, flip, preferred_element_type=F32).reshape(blocks, 8, cols)

    def finish(step, carry):
        first = (blocks // CHUNK - 1 - step) * CHUNK
        part = pl.ds(first, CHUNK)
        x = widen(xgot[part])
        s0 = jnp.concatenate(
            [r32[blocks - 1 - first - i][None] for i in range(CHUNK)], axis=0
        )
        c0 = gate[part]

        def ahead(wide, shift, after):
            turned = pltpu.roll(wide, cols - shift, 2)
            later = jnp.concatenate([turned[1:], after], axis=0)
            return jnp.where(lane < cols - shift, turned, later), turned[:1]

        s1, n0 = ahead(s0, 1, carry[0])
        s2, n1 = ahead(s0, 2, carry[1])
        c1, n2 = ahead(c0, 1, carry[2])
        c2, n3 = ahead(c0, 2, carry[3])
        grad = vt[0] * s0 + vt[1] * s1 + vt[2] * s2 + (gt[0] * c0 + gt[1] * c1 + gt[2] * c2)
        ipack[part] = narrow(grad)
        terms = [jnp.sum(t * x, axis=0, keepdims=True) for t in (s0, s1, s2, c0, c1, c2)]
        return (n0, n1, n2, n3) + tuple(a + t for a, t in zip(carry[4:], terms))

    done = lax.fori_loop(0, blocks // CHUNK, finish, (zero,) * 10)
    spot = lax.broadcasted_iota(jnp.int32, (8, LANES), 1)
    chan = lax.broadcasted_iota(jnp.int32, (8, LANES), 0)
    row = jnp.zeros((8, LANES), F32)
    for j in range(6):
        total = jnp.sum(done[4 + j][0], axis=1, keepdims=True)
        row = jnp.where(
            spot == side * 48 + j * 8 + chan, jnp.broadcast_to(total, (8, LANES)), row
        )
    twin[side] = jnp.sum(row, axis=0, keepdims=True)
    swap_t = to_seq(twin.at[side], twin.at[side], tsem.at[1], sibling)
    swap_t.start()
    keep_i = pltpu.make_async_copy(ipack.at[me], igot.at[me], own.at[1])
    keep_i.start()
    send_some(ipack, igot, isem, 1, 8)
    swap_t.wait()
    raw = twin[0] + twin[1]
    tgot[chip] = raw

    @pl.loop(1, half)
    def _(step):
        there = lax.rem(chip + step, half)
        to_seq(tgot.at[chip], tgot.at[chip], tsem.at[0], 2 * there + side).start()

    send_some(ipack, igot, isem, 8, PART)

    gp[0, :rows] = g16
    gp[0, rows:] = jnp.zeros((gp.shape[1] - rows, cols), BF16)
    gp[1, : rows - 16] = g32[1 : blocks - 1].reshape(rows - 16, cols).astype(BF16)
    gp[1, rows - 16 : rows] = jnp.concatenate(
        [g32[blocks - 1], jnp.zeros((8, cols), F32)], axis=0
    ).astype(BF16)
    gp[1, rows:] = jnp.zeros((gp.shape[1] - rows, cols), BF16)
    v16 = v32[...].reshape(rows, cols).astype(BF16)
    v_flip = lax.dot_general(
        flip, v16, (((1,), (1,)), ((), ())), preferred_element_type=F32
    ).astype(BF16)
    upper = sub_r + sub_s >= LANES - 1

    def diagonal(tile):
        turned = pltpu.roll(tile, 1, 1, stride=1, stride_axis=0)
        return jnp.sum(turned, axis=0, keepdims=True) * scale

    def lags(depth, group, carry):
        last_mid, last_corner = carry
        prods = []
        for i in range(UNROLL // 2):
            for parity in (0, 1):
                offset = pl.multiple_of((group * (UNROLL // 2) + i) * 16, 16)
                right = gp[parity, pl.ds(offset, depth), :]
                prods.append(jnp.dot(v_flip[:, :depth], right, preferred_element_type=F32))
        for i in range(UNROLL // 2):
            for parity in (0, 1):
                prod = prods[2 * i + parity]
                edge = last_corner + prod[:LANES, :LANES]
                mid = prod[LANES:, :LANES] + prod[:LANES, LANES:]
                pair = group * (UNROLL // 2) + i
                fgs[parity, pair, :, :LANES] = diagonal(jnp.where(upper, last_mid, edge))
                fgs[parity, pair, :, LANES:] = diagonal(jnp.where(upper, edge, mid))
                last_mid, last_corner = mid, prod[LANES:, LANES:]
        return last_mid, last_corner

    carry = (jnp.zeros((LANES, LANES), F32),) * 2
    turns = blocks // UNROLL
    carry = lax.fori_loop(0, turns // 2, partial(lags, rows), carry)

    drain(tgot, half - 1, tsem.at[0, 1])
    for other in range(half):
        tall[other : other + 1, :] = tgot[other]
    every = tall[...]
    squares = jnp.sum(jnp.sum(every * every, axis=0, keepdims=True), axis=1, keepdims=True)

    @pl.when(me == lead)
    def _():
        tdp[mine] = jnp.broadcast_to(squares, (1, LANES))

        @pl.loop(1, replicas)
        def _(step):
            peer = lax.rem(mine + step, replicas)
            pltpu.make_async_remote_copy(
                src_ref=tdp.at[mine], dst_ref=tdp.at[mine],
                send_sem=dsem.at[0], recv_sem=dsem.at[1],
                device_id={"dp": peer}, device_id_type=MESH,
            ).start()

    send_some(ipack, igot, isem, PART, blocks)

    carry = lax.fori_loop(turns // 2, turns, partial(lags, rows // 2), carry)
    last_mid, last_corner = carry
    fgs[0, half, :, :LANES] = diagonal(jnp.where(upper, last_mid, last_corner))
    fgs[0, half, :, LANES:] = diagonal(jnp.where(upper, last_corner, 0.0))

    swap_f = to_seq(fgs.at[side, pl.ds(1 - side, half)], fx, fsem.at[0], sibling)
    swap_f.start()

    swap_f.wait()
    fsum[...] = fgs[1 - side, pl.ds(side, half)] + fx[...]
    keep_f = pltpu.make_async_copy(fsum.at[chip], fgot.at[chip], own.at[2])
    keep_f.start()

    @pl.loop(1, half)
    def _(step):
        there = lax.rem(chip + step, half)
        to_seq(fsum.at[there], fgot.at[chip], fsem.at[1], 2 * there + side).start()


    def share(peer):
        return to_seq(tnorm, tnorm, tsem.at[2], peer)

    @pl.when(me == lead)
    def _():
        drain(tdp, replicas - 1, dsem.at[0])
        drain(tdp, replicas - 1, dsem.at[1])
        total = tdp[0]
        for other in range(1, replicas):
            total = total + tdp[other]
        tnorm[...] = total

        @pl.loop(1, blocks)
        def _(step):
            share(lax.rem(me + step, blocks)).start()

    width = blocks * 8
    pick_k = lax.broadcasted_iota(jnp.int32, (LANES, width), 0)
    pick_l = lax.broadcasted_iota(jnp.int32, (LANES, width), 1)
    pick_l = lax.rem(pick_l, 8) + 48 * lax.rem(pick_l // 8, 2)
    own_i = lax.broadcasted_iota(jnp.int32, (half, width), 0)
    own_l = lax.broadcasted_iota(jnp.int32, (half, width), 1) // 16
    for j in range(6):
        pick = jnp.where(pick_k == 8 * j + pick_l, 1.0, 0.0)
        spread = jnp.dot(every, pick, precision=lax.Precision.HIGHEST, preferred_element_type=F32)
        line = jnp.sum(jnp.where(own_i == own_l, spread, 0.0), axis=0, keepdims=True)
        t_vmem[j : j + 1, :] = line

    @pl.when(me != lead)
    def _():
        share(lead).wait_recv()

    factor = lax.rsqrt(tnorm[:, :1] * norm + 1e-05)
    t_vmem[...] = t_vmem[...] * factor
    keep_t = pltpu.make_async_copy(t_vmem, t_out, own.at[3])
    keep_t.start()

    for keep in (keep_l, keep_i, keep_f, keep_t):
        keep.wait()
    drain(hpack, half - 1, hsem.at[0, 0])
    for ref, sems in ((xpack, xsem), (upack, usem), (lpack, lsem), (ipack, isem)):
        drain(ref, blocks - 1, sems.at[0])
    drain(tgot, half - 1, tsem.at[0, 0])

    @pl.when(me == lead)
    def _():
        @pl.loop(1, blocks)
        def _(step):
            share(lax.rem(me + step, blocks)).wait_send()

    drain(fsum, half - 1, fsem.at[1, 0])
    drain(lgot, blocks - 1, lsem.at[1])
    drain(fgot, half - 1, fsem.at[1, 1])
    drain(igot, blocks - 1, isem.at[1])


def deliver(lgot, igot, fgot, taps, lo_out, ig_out, vt_out, gt_out, f_out):
    blocks = lgot.shape[0]
    from_messages(lgot, lo_out, blocks)
    from_messages(igot, ig_out, blocks)
    for row in range(fgot.shape[0]):
        f_out[row : row + 1, :] = fgot[row]
    vt_out[...] = taps[:3]
    gt_out[...] = taps[3:]


def per_device(layer_in, cotangent, value_taps, gate_taps, long_filter):
    chans, cols = layer_in.shape
    blocks = lax.axis_size("seq")
    replicas = lax.axis_size("dp")
    half = blocks // 2
    scale = 1.0 / math.sqrt(GROUP * blocks * cols)
    norm = 1.0 / (6 * chans * replicas)
    vmem = pl.BlockSpec(memory_space=pltpu.VMEM)
    anywhere = pl.BlockSpec(memory_space=pl.ANY)
    dma = pltpu.SemaphoreType.DMA
    message = pltpu.VMEM((blocks, 16, LANES), BF16)
    wide = pltpu.VMEM((blocks, 8, cols), F32)
    lines = pltpu.VMEM((half, 1, cols), F32)
    raw = pl.pallas_call(
        partial(kernel, blocks, replicas, scale, norm),
        out_shape=(
            jax.ShapeDtypeStruct((blocks, 16, LANES), BF16),
            jax.ShapeDtypeStruct((blocks, 16, LANES), BF16),
            jax.ShapeDtypeStruct((half, 1, cols), F32),
            jax.ShapeDtypeStruct((6, chans), F32),
        ),
        in_specs=[anywhere] * 5,
        out_specs=(anywhere,) * 4,
        scratch_shapes=[
            pltpu.VMEM((chans, cols), BF16),
            pltpu.VMEM((chans, cols), BF16),
            pltpu.VMEM((half, cols), BF16),
            pltpu.VMEM((3, chans), F32),
            pltpu.VMEM((3, chans), F32),
            lines,
            pltpu.VMEM((2, half, 1, cols), F32),
            *([message] * 6),
            pltpu.VMEM((blocks, cols, cols), BF16),
            pltpu.VMEM((half + STACK // 2, 16, STACK * cols), BF16),
            pltpu.VMEM((blocks + STACK * (TURNS - 1), 8, cols), F32),
            *([wide] * 4),
            pltpu.VMEM((2, 2 * blocks * 8, cols), BF16),
            pltpu.VMEM((2, half + 1, 1, cols), F32),
            lines,
            lines,
            pltpu.VMEM((2, 1, LANES), F32),
            pltpu.VMEM((replicas, 1, LANES), F32),
            pltpu.VMEM((1, LANES), F32),
            pltpu.VMEM((half, 1, LANES), F32),
            pltpu.VMEM((half, LANES), F32),
            pltpu.VMEM((6, chans), F32),
            dma((5,)),
            dma((2, 2)),
            dma((2,)),
            dma((2,)),
            dma((2,)),
            dma((2,)),
            dma((2, 2)),
            dma((2,)),
            dma((3, 2)),
            dma((4,)),
        ],
        compiler_params=pltpu.CompilerParams(
            collective_id=0, has_side_effects=True, vmem_limit_bytes=VMEM_LIMIT
        ),
        name="hyena",
    )(layer_in, cotangent, long_filter, value_taps, gate_taps)
    return pl.pallas_call(
        deliver,
        out_shape=(
            jax.ShapeDtypeStruct((chans, cols), BF16),
            jax.ShapeDtypeStruct((chans, cols), BF16),
            jax.ShapeDtypeStruct((3, chans), F32),
            jax.ShapeDtypeStruct((3, chans), F32),
            jax.ShapeDtypeStruct((half, cols), F32),
        ),
        in_specs=[vmem] * 4,
        out_specs=(vmem,) * 5,
        compiler_params=pltpu.CompilerParams(vmem_limit_bytes=VMEM_LIMIT),
        name="deliver",
    )(*raw)


def solution(mesh):
    placed = (P("dp", "seq"), P("dp", "seq"), P(None, "dp"), P(None, "dp"), P("dp", "seq"))
    return jax.shard_map(
        per_device,
        mesh=mesh,
        in_specs=placed,
        out_specs=(P("dp", "seq"), P("dp", "seq"), P(None, "dp"), P(None, "dp"), P("dp", "seq")),
        check_vma=False,
    )
```

```python
from functools import partial
import math

import jax
import jax.numpy as jnp
from jax import lax
from jax.experimental import pallas as pl
from jax.experimental.pallas import tpu as pltpu
from jax.sharding import PartitionSpec as P

GROUP = 16
LANES = 128
STACK = 8
CHUNK = 8
UNROLL = 4
TURNS = 2
PART = 40
PLANE = 8
MESH = pl.DeviceIdType.MESH
VMEM_LIMIT = 60 * 1024 * 1024
F32 = jnp.float32
BF16 = jnp.bfloat16


def widen(tile):
    wide = tile.astype(F32)
    return jnp.concatenate([wide[:, :8], wide[:, 8:]], axis=2)


def narrow(block):
    return jnp.concatenate([block[:, :, :LANES], block[:, :, LANES:]], axis=1).astype(BF16)


def to_messages(rows_ref, message_ref, blocks):
    @pl.loop(0, blocks // 2)
    def _(pair):
        rows = pl.ds(pl.multiple_of(pair * 16, 16), 16)
        wide = rows_ref[rows, :].astype(F32)
        message_ref[pl.ds(2 * pair, 2)] = narrow(wide.reshape(2, 8, 2 * LANES))


def from_messages(message_ref, rows_ref, blocks):
    @pl.loop(0, blocks // 2)
    def _(pair):
        rows = pl.ds(pl.multiple_of(pair * 16, 16), 16)
        wide = widen(message_ref[pl.ds(2 * pair, 2)])
        rows_ref[rows, :] = wide.reshape(16, 2 * LANES).astype(BF16)


def column(taps_ref, row, start):
    width = taps_ref.shape[1]
    wide = jnp.broadcast_to(taps_ref[row : row + 1, :], (8, width))
    lane = lax.broadcasted_iota(jnp.int32, (8, width), 1)
    chan = lax.broadcasted_iota(jnp.int32, (8, width), 0)
    return jnp.sum(jnp.where(lane == start + chan, wide, 0.0), axis=1, keepdims=True)


def fill_stack(load, stack, blocks, cols):
    for shift in range(2, STACK):
        stack[: shift // 2, :, shift * cols : (shift + 1) * cols] = jnp.zeros(
            (shift // 2, 16, cols), BF16
        )

    def body(pair, before):
        one, two = load(2 * pair), load(2 * pair + 1)
        even = jnp.concatenate([one, two], axis=0).astype(BF16)
        odd = jnp.concatenate([before, one], axis=0).astype(BF16)
        for shift in range(STACK):
            stack[pair + shift // 2, :, shift * cols : (shift + 1) * cols] = odd if shift % 2 else even
        return two

    lax.fori_loop(0, blocks // 2, body, jnp.zeros((8, cols), F32))


def long_conv(stack, toep, acc, blocks, cols):
    turns = blocks // STACK
    acc[...] = jnp.zeros(acc.shape, F32)
    for start in range(0, turns, TURNS):
        depth = blocks - start * STACK
        left = stack[: depth // 2].reshape(depth * 8, STACK * cols)

        @pl.loop(start, start + TURNS)
        def _(turn):
            first = turn * STACK
            right = toep[pl.ds(first, STACK)].reshape(STACK * cols, cols)
            part = jnp.dot(left, right, preferred_element_type=F32).reshape(depth, 8, cols)
            acc[pl.ds(first, depth)] += part


def kernel(
    blocks, replicas, scale, norm,
    x_hbm, u_hbm, h_hbm, vt_hbm, gt_hbm,
    lgot, igot, fgot, t_out,
    x_in, u_in, h_in, vt_ref, gt_ref,
    hpack, hgot, xpack, xgot, upack, ugot, lpack, ipack,
    toep, stack, acc, v32, g32, r32, gate, gp,
    fgs, fx, fsum, twin, tdp, tnorm, tgot, tall, t_vmem,
    loads, hsem, xsem, usem, lsem, isem, fsem, dsem, tsem, own,
):
    cols = x_hbm.shape[1]
    half = blocks // 2
    levels = blocks // PLANE
    rows = blocks * 8
    me = lax.axis_index("seq")
    mine = lax.axis_index("dp")
    side = lax.rem(me, 2)
    chip = me // 2
    sibling = me + 1 - 2 * side

    barrier = pltpu.get_barrier_semaphore()

    @pl.loop(1, blocks)
    def _(step):
        peer = lax.rem(me + step, blocks)
        pl.semaphore_signal(barrier, inc=1, device_id={"seq": peer}, device_id_type=MESH)

    lead = half

    @pl.when(me == lead)
    def _():
        @pl.loop(1, replicas)
        def _(step):
            peer = lax.rem(mine + step, replicas)
            pl.semaphore_signal(barrier, inc=1, device_id={"dp": peer}, device_id_type=MESH)

    pairs = ((h_hbm, h_in), (x_hbm, x_in), (u_hbm, u_in), (vt_hbm, vt_ref), (gt_hbm, gt_ref))
    fetched = [pltpu.make_async_copy(a, b, loads.at[i]) for i, (a, b) in enumerate(pairs)]
    for copy in fetched:
        copy.start()

    def to_seq(source, target, sems, peer):
        return pltpu.make_async_remote_copy(
            src_ref=source, dst_ref=target, send_sem=sems.at[0], recv_sem=sems.at[1],
            device_id={"seq": peer}, device_id_type=MESH,
        )

    def send_some(pack, got, sems, first, last):
        @pl.loop(first, last)
        def _(step):
            peer = lax.rem(me + step, blocks)
            to_seq(pack.at[peer], got.at[me], sems, peer).start()

    def drain(ref, count, sem):
        part = ref.at[pl.ds(0, count)]
        pltpu.make_async_copy(part, part, sem).wait()

    fetched[0].wait()
    taps = h_in[...].astype(F32)
    for row in range(half):
        hpack[row] = taps[row : row + 1]
    hgot[side, chip] = hpack[chip]
    fetched[1].wait()
    to_messages(x_in, xpack, blocks)
    xgot[me] = xpack[me]
    fetched[2].wait()
    to_messages(u_in, upack, blocks)
    ugot[me] = upack[me]
    pl.semaphore_wait(barrier, blocks - 1 + jnp.where(me == lead, replicas - 1, 0))

    @pl.loop(1, half)
    def _(step):
        there = lax.rem(chip + step, half)
        to_seq(hpack.at[there], hgot.at[side, chip], hsem.at[0], 2 * there + side).start()

    send_some(xpack, xgot, xsem, 1, blocks)
    drain(hgot.at[side], half - 1, hsem.at[0, 1])
    swap_h = to_seq(hgot.at[side], hgot.at[side], hsem.at[1], sibling)
    swap_h.start()
    send_some(upack, ugot, usem, 1, blocks)

    fetched[3].wait()
    fetched[4].wait()
    vt = [jnp.broadcast_to(column(vt_ref, j, me * 8), (8, cols))[None] for j in range(3)]
    gt = [jnp.broadcast_to(column(gt_ref, j, me * 8), (8, cols))[None] for j in range(3)]
    lane = lax.broadcasted_iota(jnp.int32, (CHUNK, 8, cols), 2)
    sub_r = lax.broadcasted_iota(jnp.int32, (LANES, LANES), 0)
    sub_s = lax.broadcasted_iota(jnp.int32, (LANES, LANES), 1)
    full_r = lax.broadcasted_iota(jnp.int32, (cols, cols), 0)
    full_s = lax.broadcasted_iota(jnp.int32, (cols, cols), 1)
    flip = jnp.where(full_r + full_s == cols - 1, 1.0, 0.0).astype(BF16)
    zero = jnp.zeros((1, 8, cols), F32)
    swap_h.wait()

    def skew(block, part):
        row = hgot[lax.rem(block, 2), block // 2, :, part * LANES : (part + 1) * LANES]
        return pltpu.roll(jnp.broadcast_to(row, (LANES, LANES)), 0, 1, stride=1, stride_axis=0)

    def build(group, carry):
        last_skew, last_edge = carry
        for i in range(UNROLL):
            block = group * UNROLL + i
            one, two = skew(block, 0), skew(block, 1)
            mid = jnp.where(sub_s >= sub_r, one, last_skew).astype(BF16)
            edge = jnp.where(sub_s >= sub_r, two, one).astype(BF16)
            toep[block, :LANES, :LANES] = mid
            toep[block, LANES:, LANES:] = mid
            toep[block, :LANES, LANES:] = edge
            toep[block, LANES:, :LANES] = last_edge
            last_skew, last_edge = two, edge
        return last_skew, last_edge

    lax.fori_loop(
        0,
        blocks // UNROLL,
        build,
        (jnp.zeros((LANES, LANES), F32), jnp.zeros((LANES, LANES), BF16)),
    )

    drain(xgot, blocks - 1, xsem.at[1])

    def short(chunk, carry):
        part = pl.ds(chunk * CHUNK, CHUNK)
        x = widen(xgot[part])
        roll1, roll2 = pltpu.roll(x, 1, 2), pltpu.roll(x, 2, 2)
        one = jnp.where(lane < 1, jnp.concatenate([carry[0], roll1[:-1]], axis=0), roll1)
        two = jnp.where(lane < 2, jnp.concatenate([carry[1], roll2[:-1]], axis=0), roll2)
        v32[part] = vt[0] * x + vt[1] * one + vt[2] * two
        gate[part] = gt[0] * x + gt[1] * one + gt[2] * two
        return roll1[-1:], roll2[-1:]

    lax.fori_loop(0, blocks // CHUNK, short, (zero, zero))
    fill_stack(lambda block: v32[block], stack, blocks, cols)
    long_conv(stack, toep, acc, blocks, cols)

    @pl.loop(0, blocks // CHUNK)
    def _(chunk):
        part = pl.ds(chunk * CHUNK, CHUNK)
        conv = acc[part].astype(BF16).astype(F32)
        acc[part] = conv
        lpack[part] = narrow(gate[part] * conv)

    keep_l = pltpu.make_async_copy(lpack.at[me], lgot.at[me], own.at[0])
    keep_l.start()
    send_some(lpack, lgot, lsem, 1, blocks)

    drain(ugot, blocks - 1, usem.at[1])

    @pl.loop(0, blocks // CHUNK)
    def _(chunk):
        part = pl.ds(chunk * CHUNK, CHUNK)
        u = widen(ugot[part])
        g32[part] = gate[part] * u
        gate[part] = (acc[part] * u).astype(BF16).astype(F32)

    g16 = g32[...].reshape(rows, cols).astype(BF16)
    r32[...] = jnp.dot(g16, flip, preferred_element_type=F32).reshape(blocks, 8, cols)
    fill_stack(lambda block: r32[blocks - 1 - block], stack, blocks, cols)
    long_conv(stack, toep, acc, blocks, cols)
    back = acc[:blocks].reshape(rows, cols).astype(BF16)
    r32[...] = jnp.dot(back, flip, preferred_element_type=F32).reshape(blocks, 8, cols)

    def finish(step, carry):
        first = (blocks // CHUNK - 1 - step) * CHUNK
        part = pl.ds(first, CHUNK)
        x = widen(xgot[part])
        s0 = jnp.concatenate(
            [r32[blocks - 1 - first - i][None] for i in range(CHUNK)], axis=0
        )
        c0 = gate[part]

        def ahead(wide, shift, after):
            turned = pltpu.roll(wide, cols - shift, 2)
            later = jnp.concatenate([turned[1:], after], axis=0)
            return jnp.where(lane < cols - shift, turned, later), turned[:1]

        s1, n0 = ahead(s0, 1, carry[0])
        s2, n1 = ahead(s0, 2, carry[1])
        c1, n2 = ahead(c0, 1, carry[2])
        c2, n3 = ahead(c0, 2, carry[3])
        grad = vt[0] * s0 + vt[1] * s1 + vt[2] * s2 + (gt[0] * c0 + gt[1] * c1 + gt[2] * c2)
        ipack[part] = narrow(grad)
        terms = [jnp.sum(t * x, axis=0, keepdims=True) for t in (s0, s1, s2, c0, c1, c2)]
        return (n0, n1, n2, n3) + tuple(a + t for a, t in zip(carry[4:], terms))

    done = lax.fori_loop(0, blocks // CHUNK, finish, (zero,) * 10)
    spot = lax.broadcasted_iota(jnp.int32, (8, LANES), 1)
    chan = lax.broadcasted_iota(jnp.int32, (8, LANES), 0)
    row = jnp.zeros((8, LANES), F32)
    for j in range(6):
        total = jnp.sum(done[4 + j][0], axis=1, keepdims=True)
        row = jnp.where(
            spot == side * 48 + j * 8 + chan, jnp.broadcast_to(total, (8, LANES)), row
        )
    twin[side] = jnp.sum(row, axis=0, keepdims=True)
    swap_t = to_seq(twin.at[side], twin.at[side], tsem.at[1], sibling)
    swap_t.start()
    keep_i = pltpu.make_async_copy(ipack.at[me], igot.at[me], own.at[1])
    keep_i.start()
    send_some(ipack, igot, isem, 1, 8)
    swap_t.wait()
    raw = twin[0] + twin[1]
    tgot[chip] = raw

    @pl.loop(1, half)
    def _(step):
        there = lax.rem(chip + step, half)
        to_seq(tgot.at[chip], tgot.at[chip], tsem.at[0], 2 * there + side).start()

    send_some(ipack, igot, isem, 8, PART)

    gp[0, :rows] = g16
    gp[0, rows:] = jnp.zeros((gp.shape[1] - rows, cols), BF16)
    gp[1, : rows - 16] = g32[1 : blocks - 1].reshape(rows - 16, cols).astype(BF16)
    gp[1, rows - 16 : rows] = jnp.concatenate(
        [g32[blocks - 1], jnp.zeros((8, cols), F32)], axis=0
    ).astype(BF16)
    gp[1, rows:] = jnp.zeros((gp.shape[1] - rows, cols), BF16)
    v16 = v32[...].reshape(rows, cols).astype(BF16)
    v_flip = lax.dot_general(
        flip, v16, (((1,), (1,)), ((), ())), preferred_element_type=F32
    ).astype(BF16)
    upper = sub_r + sub_s >= LANES - 1

    def diagonal(tile):
        turned = pltpu.roll(tile, 1, 1, stride=1, stride_axis=0)
        return jnp.sum(turned, axis=0, keepdims=True) * scale

    def lags(depth, group, carry):
        last_mid, last_corner = carry
        prods = []
        for i in range(UNROLL // 2):
            for parity in (0, 1):
                offset = pl.multiple_of((group * (UNROLL // 2) + i) * 16, 16)
                right = gp[parity, pl.ds(offset, depth), :]
                prods.append(jnp.dot(v_flip[:, :depth], right, preferred_element_type=F32))
        for i in range(UNROLL // 2):
            for parity in (0, 1):
                prod = prods[2 * i + parity]
                edge = last_corner + prod[:LANES, :LANES]
                mid = prod[LANES:, :LANES] + prod[:LANES, LANES:]
                block = group * UNROLL + 2 * i - 1 + parity + PLANE
                spot, level = lax.rem(block, PLANE), block // PLANE
                fgs[spot, level, :, :LANES] = diagonal(jnp.where(upper, last_mid, edge))
                fgs[spot, level, :, LANES:] = diagonal(jnp.where(upper, edge, mid))
                last_mid, last_corner = mid, prod[LANES:, LANES:]
        return last_mid, last_corner

    carry = (jnp.zeros((LANES, LANES), F32),) * 2
    turns = blocks // UNROLL
    carry = lax.fori_loop(0, turns // 2, partial(lags, rows), carry)

    drain(tgot, half - 1, tsem.at[0, 1])
    for other in range(half):
        tall[other : other + 1, :] = tgot[other]
    every = tall[...]
    squares = jnp.sum(jnp.sum(every * every, axis=0, keepdims=True), axis=1, keepdims=True)

    @pl.when(me == lead)
    def _():
        tdp[mine] = jnp.broadcast_to(squares, (1, LANES))

        @pl.loop(1, replicas)
        def _(step):
            peer = lax.rem(mine + step, replicas)
            pltpu.make_async_remote_copy(
                src_ref=tdp.at[mine], dst_ref=tdp.at[mine],
                send_sem=dsem.at[0], recv_sem=dsem.at[1],
                device_id={"dp": peer}, device_id_type=MESH,
            ).start()

    send_some(ipack, igot, isem, PART, blocks)

    carry = lax.fori_loop(turns // 2, turns, partial(lags, rows // 2), carry)
    last_mid, last_corner = carry
    fgs[PLANE - 1, levels, :, :LANES] = diagonal(jnp.where(upper, last_mid, last_corner))
    fgs[PLANE - 1, levels, :, LANES:] = diagonal(jnp.where(upper, last_corner, 0.0))

    seat, floor = lax.rem(me, PLANE), me // PLANE

    @pl.loop(1, PLANE)
    def _(step):
        there = lax.rem(seat + step, PLANE)
        source = fgs.at[there, pl.ds(1, levels)]
        to_seq(source, fx.at[seat], fsem.at[0], floor * PLANE + there).start()

    width = blocks * 8
    pick_k = lax.broadcasted_iota(jnp.int32, (LANES, width), 0)
    pick_l = lax.broadcasted_iota(jnp.int32, (LANES, width), 1)
    pick_l = lax.rem(pick_l, 8) + 48 * lax.rem(pick_l // 8, 2)
    own_i = lax.broadcasted_iota(jnp.int32, (half, width), 0)
    own_l = lax.broadcasted_iota(jnp.int32, (half, width), 1) // 16
    for j in range(6):
        pick = jnp.where(pick_k == 8 * j + pick_l, 1.0, 0.0)
        spread = jnp.dot(every, pick, precision=lax.Precision.HIGHEST, preferred_element_type=F32)
        line = jnp.sum(jnp.where(own_i == own_l, spread, 0.0), axis=0, keepdims=True)
        t_vmem[j : j + 1, :] = line

    fx[seat] = fgs[seat, pl.ds(1, levels)]
    drain(fx, PLANE - 1, fsem.at[0, 1])
    for x in range(PLANE // 2):
        fsum[:, x] = fx[2 * x] + fx[2 * x + 1]
    mine_f = pl.ds(floor * (PLANE // 2), PLANE // 2)
    keep_f = pltpu.make_async_copy(fsum.at[floor], fgot.at[mine_f], own.at[2])
    keep_f.start()

    @pl.loop(1, levels)
    def _(step):
        there = lax.rem(floor + step, levels)
        to_seq(fsum.at[there], fgot.at[mine_f], fsem.at[1], there * PLANE + seat).start()

    def share(peer):
        return to_seq(tnorm, tnorm, tsem.at[2], peer)

    def each_floor(act):
        @pl.loop(1, levels)
        def _(step):
            act(share(lax.rem(floor + step, levels) * PLANE + seat))

    def each_seat(act):
        @pl.loop(1, PLANE)
        def _(step):
            act(share(floor * PLANE + lax.rem(seat + step, PLANE)))

    @pl.when(me == lead)
    def _():
        drain(tdp, replicas - 1, dsem.at[0])
        drain(tdp, replicas - 1, dsem.at[1])
        total = tdp[0]
        for other in range(1, replicas):
            total = total + tdp[other]
        tnorm[...] = total
        each_floor(lambda copy: copy.start())

    @pl.when(me != lead)
    def _():
        share(lead).wait_recv()

    @pl.when(seat == lead % PLANE)
    def _():
        each_seat(lambda copy: copy.start())

    factor = lax.rsqrt(tnorm[:, :1] * norm + 1e-05)
    t_vmem[...] = t_vmem[...] * factor
    keep_t = pltpu.make_async_copy(t_vmem, t_out, own.at[3])
    keep_t.start()

    for keep in (keep_l, keep_i, keep_f, keep_t):
        keep.wait()
    drain(hpack, half - 1, hsem.at[0, 0])
    for ref, sems in ((xpack, xsem), (upack, usem), (lpack, lsem), (ipack, isem)):
        drain(ref, blocks - 1, sems.at[0])
    drain(tgot, half - 1, tsem.at[0, 0])

    @pl.when(me == lead)
    def _():
        each_floor(lambda copy: copy.wait_send())

    @pl.when(seat == lead % PLANE)
    def _():
        each_seat(lambda copy: copy.wait_send())

    drain(fx, PLANE - 1, fsem.at[0, 0])
    drain(fsum, levels - 1, fsem.at[1, 0])
    drain(lgot, blocks - 1, lsem.at[1])
    drain(fgot, (levels - 1) * (PLANE // 2), fsem.at[1, 1])
    drain(igot, blocks - 1, isem.at[1])


def deliver(lgot, igot, fgot, taps, lo_out, ig_out, vt_out, gt_out, f_out):
    blocks = lgot.shape[0]
    from_messages(lgot, lo_out, blocks)
    from_messages(igot, ig_out, blocks)
    for row in range(fgot.shape[0]):
        f_out[row : row + 1, :] = fgot[row]
    vt_out[...] = taps[:3]
    gt_out[...] = taps[3:]


def per_device(layer_in, cotangent, value_taps, gate_taps, long_filter):
    chans, cols = layer_in.shape
    blocks = lax.axis_size("seq")
    replicas = lax.axis_size("dp")
    half = blocks // 2
    scale = 1.0 / math.sqrt(GROUP * blocks * cols)
    norm = 1.0 / (6 * chans * replicas)
    vmem = pl.BlockSpec(memory_space=pltpu.VMEM)
    anywhere = pl.BlockSpec(memory_space=pl.ANY)
    dma = pltpu.SemaphoreType.DMA
    message = pltpu.VMEM((blocks, 16, LANES), BF16)
    wide = pltpu.VMEM((blocks, 8, cols), F32)
    lines = pltpu.VMEM((half, 1, cols), F32)
    raw = pl.pallas_call(
        partial(kernel, blocks, replicas, scale, norm),
        out_shape=(
            jax.ShapeDtypeStruct((blocks, 16, LANES), BF16),
            jax.ShapeDtypeStruct((blocks, 16, LANES), BF16),
            jax.ShapeDtypeStruct((half, 1, cols), F32),
            jax.ShapeDtypeStruct((6, chans), F32),
        ),
        in_specs=[anywhere] * 5,
        out_specs=(anywhere,) * 4,
        scratch_shapes=[
            pltpu.VMEM((chans, cols), BF16),
            pltpu.VMEM((chans, cols), BF16),
            pltpu.VMEM((half, cols), BF16),
            pltpu.VMEM((3, chans), F32),
            pltpu.VMEM((3, chans), F32),
            lines,
            pltpu.VMEM((2, half, 1, cols), F32),
            *([message] * 6),
            pltpu.VMEM((blocks, cols, cols), BF16),
            pltpu.VMEM((half + STACK // 2, 16, STACK * cols), BF16),
            pltpu.VMEM((blocks + STACK * (TURNS - 1), 8, cols), F32),
            *([wide] * 4),
            pltpu.VMEM((2, 2 * blocks * 8, cols), BF16),
            pltpu.VMEM((PLANE, blocks // PLANE + 1, 1, cols), F32),
            pltpu.VMEM((PLANE, blocks // PLANE, 1, cols), F32),
            pltpu.VMEM((blocks // PLANE, PLANE // 2, 1, cols), F32),
            pltpu.VMEM((2, 1, LANES), F32),
            pltpu.VMEM((replicas, 1, LANES), F32),
            pltpu.VMEM((1, LANES), F32),
            pltpu.VMEM((half, 1, LANES), F32),
            pltpu.VMEM((half, LANES), F32),
            pltpu.VMEM((6, chans), F32),
            dma((5,)),
            dma((2, 2)),
            dma((2,)),
            dma((2,)),
            dma((2,)),
            dma((2,)),
            dma((2, 2)),
            dma((2,)),
            dma((3, 2)),
            dma((4,)),
        ],
        compiler_params=pltpu.CompilerParams(
            collective_id=0, has_side_effects=True, vmem_limit_bytes=VMEM_LIMIT
        ),
        name="hyena",
    )(layer_in, cotangent, long_filter, value_taps, gate_taps)
    return pl.pallas_call(
        deliver,
        out_shape=(
            jax.ShapeDtypeStruct((chans, cols), BF16),
            jax.ShapeDtypeStruct((chans, cols), BF16),
            jax.ShapeDtypeStruct((3, chans), F32),
            jax.ShapeDtypeStruct((3, chans), F32),
            jax.ShapeDtypeStruct((half, cols), F32),
        ),
        in_specs=[vmem] * 4,
        out_specs=(vmem,) * 5,
        compiler_params=pltpu.CompilerParams(vmem_limit_bytes=VMEM_LIMIT),
        name="deliver",
    )(*raw)


def solution(mesh):
    placed = (P("dp", "seq"), P("dp", "seq"), P(None, "dp"), P(None, "dp"), P("dp", "seq"))
    return jax.shard_map(
        per_device,
        mesh=mesh,
        in_specs=placed,
        out_specs=(P("dp", "seq"), P("dp", "seq"), P(None, "dp"), P(None, "dp"), P("dp", "seq")),
        check_vma=False,
    )
```

```python
from functools import partial
import math

import jax
import jax.numpy as jnp
from jax import lax
from jax.experimental import pallas as pl
from jax.experimental.pallas import tpu as pltpu
from jax.sharding import PartitionSpec as P

GROUP = 16
LANES = 128
STACK = 8
CHUNK = 8
UNROLL = 4
TURNS = 2
PART = 40
MESH = pl.DeviceIdType.MESH
VMEM_LIMIT = 60 * 1024 * 1024
F32 = jnp.float32
BF16 = jnp.bfloat16


def widen(tile):
    wide = tile.astype(F32)
    return jnp.concatenate([wide[:, :8], wide[:, 8:]], axis=2)


def narrow(block):
    return jnp.concatenate([block[:, :, :LANES], block[:, :, LANES:]], axis=1).astype(BF16)


def to_messages(rows_ref, message_ref, blocks):
    @pl.loop(0, blocks // 2)
    def _(pair):
        rows = pl.ds(pl.multiple_of(pair * 16, 16), 16)
        wide = rows_ref[rows, :].astype(F32)
        message_ref[pl.ds(2 * pair, 2)] = narrow(wide.reshape(2, 8, 2 * LANES))


def from_messages(message_ref, rows_ref, blocks):
    @pl.loop(0, blocks // 2)
    def _(pair):
        rows = pl.ds(pl.multiple_of(pair * 16, 16), 16)
        wide = widen(message_ref[pl.ds(2 * pair, 2)])
        rows_ref[rows, :] = wide.reshape(16, 2 * LANES).astype(BF16)


def column(taps_ref, row, start):
    width = taps_ref.shape[1]
    wide = jnp.broadcast_to(taps_ref[row : row + 1, :], (8, width))
    lane = lax.broadcasted_iota(jnp.int32, (8, width), 1)
    chan = lax.broadcasted_iota(jnp.int32, (8, width), 0)
    return jnp.sum(jnp.where(lane == start + chan, wide, 0.0), axis=1, keepdims=True)


def fill_stack(load, stack, blocks, cols):
    for shift in range(2, STACK):
        stack[: shift // 2, :, shift * cols : (shift + 1) * cols] = jnp.zeros(
            (shift // 2, 16, cols), BF16
        )

    def body(pair, before):
        one, two = load(2 * pair), load(2 * pair + 1)
        even = jnp.concatenate([one, two], axis=0).astype(BF16)
        odd = jnp.concatenate([before, one], axis=0).astype(BF16)
        for shift in range(STACK):
            stack[pair + shift // 2, :, shift * cols : (shift + 1) * cols] = odd if shift % 2 else even
        return two

    lax.fori_loop(0, blocks // 2, body, jnp.zeros((8, cols), F32))


def long_conv(stack, toep, acc, blocks, cols):
    turns = blocks // STACK
    acc[...] = jnp.zeros(acc.shape, F32)
    for start in range(0, turns, TURNS):
        depth = blocks - start * STACK
        left = stack[: depth // 2].reshape(depth * 8, STACK * cols)

        @pl.loop(start, start + TURNS)
        def _(turn):
            first = turn * STACK
            right = toep[pl.ds(first, STACK)].reshape(STACK * cols, cols)
            part = jnp.dot(left, right, preferred_element_type=F32).reshape(depth, 8, cols)
            acc[pl.ds(first, depth)] += part


def kernel(
    blocks, replicas, scale, norm,
    x_hbm, u_hbm, h_hbm, vt_hbm, gt_hbm,
    lgot, igot, fgot, t_out,
    x_in, u_in, h_in, vt_ref, gt_ref,
    hpack, hgot, xpack, xgot, upack, ugot, lpack, ipack,
    toep, stack, acc, v32, g32, r32, gate, gp,
    fgs, fx, fsum, twin, tdp, tnorm, tgot, tall, t_vmem,
    loads, hsem, xsem, usem, lsem, isem, fsem, dsem, tsem, own,
):
    cols = x_hbm.shape[1]
    half = blocks // 2
    rows = blocks * 8
    me = lax.axis_index("seq")
    mine = lax.axis_index("dp")
    side = lax.rem(me, 2)
    chip = me // 2
    sibling = me + 1 - 2 * side

    barrier = pltpu.get_barrier_semaphore()

    @pl.loop(1, blocks)
    def _(step):
        peer = lax.rem(me + step, blocks)
        pl.semaphore_signal(barrier, inc=1, device_id={"seq": peer}, device_id_type=MESH)

    lead = half

    @pl.when(me == lead)
    def _():
        @pl.loop(1, replicas)
        def _(step):
            peer = lax.rem(mine + step, replicas)
            pl.semaphore_signal(barrier, inc=1, device_id={"dp": peer}, device_id_type=MESH)

    pairs = ((h_hbm, h_in), (x_hbm, x_in), (u_hbm, u_in), (vt_hbm, vt_ref), (gt_hbm, gt_ref))
    fetched = [pltpu.make_async_copy(a, b, loads.at[i]) for i, (a, b) in enumerate(pairs)]
    for copy in fetched:
        copy.start()

    def to_seq(source, target, sems, peer):
        return pltpu.make_async_remote_copy(
            src_ref=source, dst_ref=target, send_sem=sems.at[0], recv_sem=sems.at[1],
            device_id={"seq": peer}, device_id_type=MESH,
        )

    def send_some(pack, got, sems, first, last):
        @pl.loop(first, last)
        def _(step):
            away = (step + 1) // 2
            peer = lax.rem(me + jnp.where(lax.rem(step, 2) == 1, away, blocks - away), blocks)
            to_seq(pack.at[peer], got.at[me], sems, peer).start()

    def drain(ref, count, sem):
        part = ref.at[pl.ds(0, count)]
        pltpu.make_async_copy(part, part, sem).wait()

    fetched[0].wait()
    taps = h_in[...].astype(F32)
    for row in range(half):
        hpack[row] = taps[row : row + 1]
    hgot[side, chip] = hpack[chip]
    fetched[1].wait()
    to_messages(x_in, xpack, blocks)
    xgot[me] = xpack[me]
    fetched[2].wait()
    to_messages(u_in, upack, blocks)
    ugot[me] = upack[me]
    pl.semaphore_wait(barrier, blocks - 1 + jnp.where(me == lead, replicas - 1, 0))

    @pl.loop(1, half)
    def _(step):
        there = lax.rem(chip + step, half)
        to_seq(hpack.at[there], hgot.at[side, chip], hsem.at[0], 2 * there + side).start()

    send_some(xpack, xgot, xsem, 1, blocks)
    drain(hgot.at[side], half - 1, hsem.at[0, 1])
    swap_h = to_seq(hgot.at[side], hgot.at[side], hsem.at[1], sibling)
    swap_h.start()
    send_some(upack, ugot, usem, 1, blocks)

    fetched[3].wait()
    fetched[4].wait()
    vt = [jnp.broadcast_to(column(vt_ref, j, me * 8), (8, cols))[None] for j in range(3)]
    gt = [jnp.broadcast_to(column(gt_ref, j, me * 8), (8, cols))[None] for j in range(3)]
    lane = lax.broadcasted_iota(jnp.int32, (CHUNK, 8, cols), 2)
    sub_r = lax.broadcasted_iota(jnp.int32, (LANES, LANES), 0)
    sub_s = lax.broadcasted_iota(jnp.int32, (LANES, LANES), 1)
    full_r = lax.broadcasted_iota(jnp.int32, (cols, cols), 0)
    full_s = lax.broadcasted_iota(jnp.int32, (cols, cols), 1)
    flip = jnp.where(full_r + full_s == cols - 1, 1.0, 0.0).astype(BF16)
    zero = jnp.zeros((1, 8, cols), F32)
    swap_h.wait()

    def skew(block, part):
        row = hgot[lax.rem(block, 2), block // 2, :, part * LANES : (part + 1) * LANES]
        return pltpu.roll(jnp.broadcast_to(row, (LANES, LANES)), 0, 1, stride=1, stride_axis=0)

    def build(group, carry):
        last_skew, last_edge = carry
        for i in range(UNROLL):
            block = group * UNROLL + i
            one, two = skew(block, 0), skew(block, 1)
            mid = jnp.where(sub_s >= sub_r, one, last_skew).astype(BF16)
            edge = jnp.where(sub_s >= sub_r, two, one).astype(BF16)
            toep[block, :LANES, :LANES] = mid
            toep[block, LANES:, LANES:] = mid
            toep[block, :LANES, LANES:] = edge
            toep[block, LANES:, :LANES] = last_edge
            last_skew, last_edge = two, edge
        return last_skew, last_edge

    lax.fori_loop(
        0,
        blocks // UNROLL,
        build,
        (jnp.zeros((LANES, LANES), F32), jnp.zeros((LANES, LANES), BF16)),
    )

    drain(xgot, blocks - 1, xsem.at[1])

    def short(chunk, carry):
        part = pl.ds(chunk * CHUNK, CHUNK)
        x = widen(xgot[part])
        roll1, roll2 = pltpu.roll(x, 1, 2), pltpu.roll(x, 2, 2)
        one = jnp.where(lane < 1, jnp.concatenate([carry[0], roll1[:-1]], axis=0), roll1)
        two = jnp.where(lane < 2, jnp.concatenate([carry[1], roll2[:-1]], axis=0), roll2)
        v32[part] = vt[0] * x + vt[1] * one + vt[2] * two
        gate[part] = gt[0] * x + gt[1] * one + gt[2] * two
        return roll1[-1:], roll2[-1:]

    lax.fori_loop(0, blocks // CHUNK, short, (zero, zero))
    fill_stack(lambda block: v32[block], stack, blocks, cols)
    long_conv(stack, toep, acc, blocks, cols)

    @pl.loop(0, blocks // CHUNK)
    def _(chunk):
        part = pl.ds(chunk * CHUNK, CHUNK)
        conv = acc[part].astype(BF16).astype(F32)
        acc[part] = conv
        lpack[part] = narrow(gate[part] * conv)

    keep_l = pltpu.make_async_copy(lpack.at[me], lgot.at[me], own.at[0])
    keep_l.start()
    send_some(lpack, lgot, lsem, 1, blocks)

    drain(ugot, blocks - 1, usem.at[1])

    @pl.loop(0, blocks // CHUNK)
    def _(chunk):
        part = pl.ds(chunk * CHUNK, CHUNK)
        u = widen(ugot[part])
        g32[part] = gate[part] * u
        gate[part] = (acc[part] * u).astype(BF16).astype(F32)

    g16 = g32[...].reshape(rows, cols).astype(BF16)
    r32[...] = jnp.dot(g16, flip, preferred_element_type=F32).reshape(blocks, 8, cols)
    fill_stack(lambda block: r32[blocks - 1 - block], stack, blocks, cols)
    long_conv(stack, toep, acc, blocks, cols)
    back = acc[:blocks].reshape(rows, cols).astype(BF16)
    r32[...] = jnp.dot(back, flip, preferred_element_type=F32).reshape(blocks, 8, cols)

    def finish(step, carry):
        first = (blocks // CHUNK - 1 - step) * CHUNK
        part = pl.ds(first, CHUNK)
        x = widen(xgot[part])
        s0 = jnp.concatenate(
            [r32[blocks - 1 - first - i][None] for i in range(CHUNK)], axis=0
        )
        c0 = gate[part]

        def ahead(wide, shift, after):
            turned = pltpu.roll(wide, cols - shift, 2)
            later = jnp.concatenate([turned[1:], after], axis=0)
            return jnp.where(lane < cols - shift, turned, later), turned[:1]

        s1, n0 = ahead(s0, 1, carry[0])
        s2, n1 = ahead(s0, 2, carry[1])
        c1, n2 = ahead(c0, 1, carry[2])
        c2, n3 = ahead(c0, 2, carry[3])
        grad = vt[0] * s0 + vt[1] * s1 + vt[2] * s2 + (gt[0] * c0 + gt[1] * c1 + gt[2] * c2)
        ipack[part] = narrow(grad)
        terms = [jnp.sum(t * x, axis=0, keepdims=True) for t in (s0, s1, s2, c0, c1, c2)]
        return (n0, n1, n2, n3) + tuple(a + t for a, t in zip(carry[4:], terms))

    done = lax.fori_loop(0, blocks // CHUNK, finish, (zero,) * 10)
    spot = lax.broadcasted_iota(jnp.int32, (8, LANES), 1)
    chan = lax.broadcasted_iota(jnp.int32, (8, LANES), 0)
    row = jnp.zeros((8, LANES), F32)
    for j in range(6):
        total = jnp.sum(done[4 + j][0], axis=1, keepdims=True)
        row = jnp.where(
            spot == side * 48 + j * 8 + chan, jnp.broadcast_to(total, (8, LANES)), row
        )
    twin[side] = jnp.sum(row, axis=0, keepdims=True)
    swap_t = to_seq(twin.at[side], twin.at[side], tsem.at[1], sibling)
    swap_t.start()
    keep_i = pltpu.make_async_copy(ipack.at[me], igot.at[me], own.at[1])
    keep_i.start()
    send_some(ipack, igot, isem, 1, 8)
    swap_t.wait()
    raw = twin[0] + twin[1]
    tgot[chip] = raw

    @pl.loop(1, half)
    def _(step):
        there = lax.rem(chip + step, half)
        to_seq(tgot.at[chip], tgot.at[chip], tsem.at[0], 2 * there + side).start()

    send_some(ipack, igot, isem, 8, PART)

    gp[0, :rows] = g16
    gp[0, rows:] = jnp.zeros((gp.shape[1] - rows, cols), BF16)
    gp[1, : rows - 16] = g32[1 : blocks - 1].reshape(rows - 16, cols).astype(BF16)
    gp[1, rows - 16 : rows] = jnp.concatenate(
        [g32[blocks - 1], jnp.zeros((8, cols), F32)], axis=0
    ).astype(BF16)
    gp[1, rows:] = jnp.zeros((gp.shape[1] - rows, cols), BF16)
    v16 = v32[...].reshape(rows, cols).astype(BF16)
    v_flip = lax.dot_general(
        flip, v16, (((1,), (1,)), ((), ())), preferred_element_type=F32
    ).astype(BF16)
    upper = sub_r + sub_s >= LANES - 1

    def diagonal(tile):
        turned = pltpu.roll(tile, 1, 1, stride=1, stride_axis=0)
        return jnp.sum(turned, axis=0, keepdims=True) * scale

    def lags(depth, group, carry):
        last_mid, last_corner = carry
        prods = []
        for i in range(UNROLL // 2):
            for parity in (0, 1):
                offset = pl.multiple_of((group * (UNROLL // 2) + i) * 16, 16)
                right = gp[parity, pl.ds(offset, depth), :]
                prods.append(jnp.dot(v_flip[:, :depth], right, preferred_element_type=F32))
        for i in range(UNROLL // 2):
            for parity in (0, 1):
                prod = prods[2 * i + parity]
                edge = last_corner + prod[:LANES, :LANES]
                mid = prod[LANES:, :LANES] + prod[:LANES, LANES:]
                pair = group * (UNROLL // 2) + i
                fgs[parity, pair, :, :LANES] = diagonal(jnp.where(upper, last_mid, edge))
                fgs[parity, pair, :, LANES:] = diagonal(jnp.where(upper, edge, mid))
                last_mid, last_corner = mid, prod[LANES:, LANES:]
        return last_mid, last_corner

    carry = (jnp.zeros((LANES, LANES), F32),) * 2
    turns = blocks // UNROLL
    carry = lax.fori_loop(0, turns // 2, partial(lags, rows), carry)

    drain(tgot, half - 1, tsem.at[0, 1])
    for other in range(half):
        tall[other : other + 1, :] = tgot[other]
    every = tall[...]
    squares = jnp.sum(jnp.sum(every * every, axis=0, keepdims=True), axis=1, keepdims=True)

    @pl.when(me == lead)
    def _():
        tdp[mine] = jnp.broadcast_to(squares, (1, LANES))

        @pl.loop(1, replicas)
        def _(step):
            peer = lax.rem(mine + step, replicas)
            pltpu.make_async_remote_copy(
                src_ref=tdp.at[mine], dst_ref=tdp.at[mine],
                send_sem=dsem.at[0], recv_sem=dsem.at[1],
                device_id={"dp": peer}, device_id_type=MESH,
            ).start()

    send_some(ipack, igot, isem, PART, blocks)

    carry = lax.fori_loop(turns // 2, turns, partial(lags, rows // 2), carry)
    last_mid, last_corner = carry
    fgs[0, half, :, :LANES] = diagonal(jnp.where(upper, last_mid, last_corner))
    fgs[0, half, :, LANES:] = diagonal(jnp.where(upper, last_corner, 0.0))

    swap_f = to_seq(fgs.at[side, pl.ds(1 - side, half)], fx, fsem.at[0], sibling)
    swap_f.start()

    swap_f.wait()
    fsum[...] = fgs[1 - side, pl.ds(side, half)] + fx[...]
    keep_f = pltpu.make_async_copy(fsum.at[chip], fgot.at[chip], own.at[2])
    keep_f.start()

    @pl.loop(1, half)
    def _(step):
        there = lax.rem(chip + step, half)
        to_seq(fsum.at[there], fgot.at[chip], fsem.at[1], 2 * there + side).start()


    def share(peer):
        return to_seq(tnorm, tnorm, tsem.at[2], peer)

    @pl.when(me == lead)
    def _():
        drain(tdp, replicas - 1, dsem.at[0])
        drain(tdp, replicas - 1, dsem.at[1])
        total = tdp[0]
        for other in range(1, replicas):
            total = total + tdp[other]
        tnorm[...] = total

        @pl.loop(1, blocks)
        def _(step):
            share(lax.rem(me + step, blocks)).start()

    width = blocks * 8
    pick_k = lax.broadcasted_iota(jnp.int32, (LANES, width), 0)
    pick_l = lax.broadcasted_iota(jnp.int32, (LANES, width), 1)
    pick_l = lax.rem(pick_l, 8) + 48 * lax.rem(pick_l // 8, 2)
    own_i = lax.broadcasted_iota(jnp.int32, (half, width), 0)
    own_l = lax.broadcasted_iota(jnp.int32, (half, width), 1) // 16
    for j in range(6):
        pick = jnp.where(pick_k == 8 * j + pick_l, 1.0, 0.0)
        spread = jnp.dot(every, pick, precision=lax.Precision.HIGHEST, preferred_element_type=F32)
        line = jnp.sum(jnp.where(own_i == own_l, spread, 0.0), axis=0, keepdims=True)
        t_vmem[j : j + 1, :] = line

    @pl.when(me != lead)
    def _():
        share(lead).wait_recv()

    factor = lax.rsqrt(tnorm[:, :1] * norm + 1e-05)
    t_vmem[...] = t_vmem[...] * factor
    keep_t = pltpu.make_async_copy(t_vmem, t_out, own.at[3])
    keep_t.start()

    for keep in (keep_l, keep_i, keep_f, keep_t):
        keep.wait()
    drain(hpack, half - 1, hsem.at[0, 0])
    for ref, sems in ((xpack, xsem), (upack, usem), (lpack, lsem), (ipack, isem)):
        drain(ref, blocks - 1, sems.at[0])
    drain(tgot, half - 1, tsem.at[0, 0])

    @pl.when(me == lead)
    def _():
        @pl.loop(1, blocks)
        def _(step):
            share(lax.rem(me + step, blocks)).wait_send()

    drain(fsum, half - 1, fsem.at[1, 0])
    drain(lgot, blocks - 1, lsem.at[1])
    drain(fgot, half - 1, fsem.at[1, 1])
    drain(igot, blocks - 1, isem.at[1])


def deliver(lgot, igot, fgot, taps, lo_out, ig_out, vt_out, gt_out, f_out):
    blocks = lgot.shape[0]
    from_messages(lgot, lo_out, blocks)
    from_messages(igot, ig_out, blocks)
    for row in range(fgot.shape[0]):
        f_out[row : row + 1, :] = fgot[row]
    vt_out[...] = taps[:3]
    gt_out[...] = taps[3:]


def per_device(layer_in, cotangent, value_taps, gate_taps, long_filter):
    chans, cols = layer_in.shape
    blocks = lax.axis_size("seq")
    replicas = lax.axis_size("dp")
    half = blocks // 2
    scale = 1.0 / math.sqrt(GROUP * blocks * cols)
    norm = 1.0 / (6 * chans * replicas)
    vmem = pl.BlockSpec(memory_space=pltpu.VMEM)
    anywhere = pl.BlockSpec(memory_space=pl.ANY)
    dma = pltpu.SemaphoreType.DMA
    message = pltpu.VMEM((blocks, 16, LANES), BF16)
    wide = pltpu.VMEM((blocks, 8, cols), F32)
    lines = pltpu.VMEM((half, 1, cols), F32)
    raw = pl.pallas_call(
        partial(kernel, blocks, replicas, scale, norm),
        out_shape=(
            jax.ShapeDtypeStruct((blocks, 16, LANES), BF16),
            jax.ShapeDtypeStruct((blocks, 16, LANES), BF16),
            jax.ShapeDtypeStruct((half, 1, cols), F32),
            jax.ShapeDtypeStruct((6, chans), F32),
        ),
        in_specs=[anywhere] * 5,
        out_specs=(anywhere,) * 4,
        scratch_shapes=[
            pltpu.VMEM((chans, cols), BF16),
            pltpu.VMEM((chans, cols), BF16),
            pltpu.VMEM((half, cols), BF16),
            pltpu.VMEM((3, chans), F32),
            pltpu.VMEM((3, chans), F32),
            lines,
            pltpu.VMEM((2, half, 1, cols), F32),
            *([message] * 6),
            pltpu.VMEM((blocks, cols, cols), BF16),
            pltpu.VMEM((half + STACK // 2, 16, STACK * cols), BF16),
            pltpu.VMEM((blocks + STACK * (TURNS - 1), 8, cols), F32),
            *([wide] * 4),
            pltpu.VMEM((2, 2 * blocks * 8, cols), BF16),
            pltpu.VMEM((2, half + 1, 1, cols), F32),
            lines,
            lines,
            pltpu.VMEM((2, 1, LANES), F32),
            pltpu.VMEM((replicas, 1, LANES), F32),
            pltpu.VMEM((1, LANES), F32),
            pltpu.VMEM((half, 1, LANES), F32),
            pltpu.VMEM((half, LANES), F32),
            pltpu.VMEM((6, chans), F32),
            dma((5,)),
            dma((2, 2)),
            dma((2,)),
            dma((2,)),
            dma((2,)),
            dma((2,)),
            dma((2, 2)),
            dma((2,)),
            dma((3, 2)),
            dma((4,)),
        ],
        compiler_params=pltpu.CompilerParams(
            collective_id=0, has_side_effects=True, vmem_limit_bytes=VMEM_LIMIT
        ),
        name="hyena",
    )(layer_in, cotangent, long_filter, value_taps, gate_taps)
    return pl.pallas_call(
        deliver,
        out_shape=(
            jax.ShapeDtypeStruct((chans, cols), BF16),
            jax.ShapeDtypeStruct((chans, cols), BF16),
            jax.ShapeDtypeStruct((3, chans), F32),
            jax.ShapeDtypeStruct((3, chans), F32),
            jax.ShapeDtypeStruct((half, cols), F32),
        ),
        in_specs=[vmem] * 4,
        out_specs=(vmem,) * 5,
        compiler_params=pltpu.CompilerParams(vmem_limit_bytes=VMEM_LIMIT),
        name="deliver",
    )(*raw)


def solution(mesh):
    placed = (P("dp", "seq"), P("dp", "seq"), P(None, "dp"), P(None, "dp"), P("dp", "seq"))
    return jax.shard_map(
        per_device,
        mesh=mesh,
        in_specs=placed,
        out_specs=(P("dp", "seq"), P("dp", "seq"), P(None, "dp"), P(None, "dp"), P("dp", "seq")),
        check_vma=False,
    )
```
